128 devices in a mesh: dp: 32 (over y, x_lo, z), seq: 4 (over x_hi, core).
Axes of the slice: x: 4 (x_hi: 2, x_lo: 2; x = x_hi * 2 + x_lo), y: 4, z: 4, core: 2. Of those that a mesh axis runs over, the one named last changes fastest.
Arguments:
- layer_in: bfloat16 [64, 512, 1024], P('dp', 'seq'), may hold values from -6 to 6
- w_query: bfloat16 [1024, 1024], P(('dp', 'seq')), may hold values from -0.1875 to 0.1875
- w_key: bfloat16 [1024, 1024], P(('dp', 'seq')), may hold values from -0.1875 to 0.1875
- w_value: bfloat16 [1024, 1024], P(('dp', 'seq')), may hold values from -0.1875 to 0.1875
- w_out: bfloat16 [1024, 1024], P(('dp', 'seq')), may hold values from -1.5 to 1.5
- norm_attn: bfloat16 [1024], P(('dp', 'seq')), may hold values from 0.5 to 1.5
- norm_moe: bfloat16 [1024], P(('dp', 'seq')), may hold values from 0.5 to 1.5
- rel_table: bfloat16 [512], P(('dp', 'seq')), may hold values from -4 to 4
- w_router: bfloat16 [1024, 32], P(('dp', 'seq')), may hold values from -0.125 to 0.125
- expert_gate: bfloat16 [32, 1024, 2816], P('dp', None, 'seq'), may hold values from -0.1875 to 0.1875
- expert_up: bfloat16 [32, 1024, 2816], P('dp', None, 'seq'), may hold values from -0.1875 to 0.1875
- expert_down: bfloat16 [32, 2816, 1024], P('dp', 'seq'), may hold values from -0.109375 to 0.109375
- routes: int32 [64, 512, 2], P('dp', 'seq'), may hold values from 0 to 31, all different within a row; in each aligned block of 128 rows (0 to 127, 128 to 255, ..., all dimensions but the last counted through in order) at most 16 rows name the same one
- rel_bucket: int32 [1023], replicated, may hold values from 0 to 31, as said below
- cotangent: bfloat16 [64, 512, 1024], P('dp', 'seq'), may hold values from -6 to 6
Outputs:
- layer_out: bfloat16 [64, 512, 1024], P('dp', 'seq')
- grad_in: float32 [64, 512, 1024], P('dp', 'seq')
- grad_query: float32 [1024, 1024], P(('dp', 'seq'))
- grad_key: float32 [1024, 1024], P(('dp', 'seq'))
- grad_value: float32 [1024, 1024], P(('dp', 'seq'))
- grad_out: float32 [1024, 1024], P(('dp', 'seq'))
- grad_norm_attn: float32 [1024], P(('dp', 'seq'))
- grad_norm_moe: float32 [1024], P(('dp', 'seq'))
- grad_rel_table: float32 [512], P(('dp', 'seq'))
- grad_router: float32 [1024, 32], P(('dp', 'seq'))
- grad_gate: float32 [32, 1024, 2816], P('dp', None, 'seq')
- grad_up: float32 [32, 1024, 2816], P('dp', None, 'seq')
- grad_down: float32 [32, 2816, 1024], P('dp', 'seq')
- expert_counts: int32 [2, 32], replicated
The draws below stay inside these ranges and needn't reach their ends.
Inputs may be any that keep to these rules, and one draw needn't show every extreme that they name: `routes`: in each aligned block of 128 rows (one item's positions on one device) no expert is named by more than 16 rows; the two entries of a row differ. `rel_bucket`: 0 at offset 0; for offsets d >= 0 below 16 and for d < 0 at or above it; does not fall as |d| grows on either side.
All inputs are finite; a program needn't handle non-finite values.
Results may differ from the reference program's by a relative error of at most 0.025.
Values may be sent and summed in bfloat16 or wider, within the bound.
A program may use at most 256 MiB of HBM per device.

```python
import math
import jax
import jax.numpy as jnp
import numpy as np
from jax import lax

D = 1024
HEADS = 16
HEAD_DIM = 64
FF = 2816
BUCKETS = 32
LENGTH = 512
ITEMS_DP = 2
EXPERTS = 32
ITEMS = 64
SEQ_DEV = 128
TOK_DEV = 256
CAP = 20
ROUTE_MOST = 16
N_DP = 32
N_SEQ = 4


def draw_rel_bucket(key, part):
    key = jax.random.fold_in(key, 7)
    half = BUCKETS // 2
    breaks = jax.random.permutation(key, LENGTH - 1)[:half - 1] + 1
    offsets = jnp.arange(2 * LENGTH - 1, dtype=jnp.int32) - (LENGTH - 1)
    magnitude = jnp.abs(offsets)
    passed = jnp.sum((magnitude[:, None] >= breaks[None, :]).astype(jnp.int32), 1)
    return jnp.where(offsets < 0, half + passed, passed).astype(jnp.int32)


def levels(key, dims, split, least, largest):
    def one(position, blocks):
        draws = jax.random.uniform(jax.random.fold_in(jax.random.fold_in(key, 6), position), (blocks,), jnp.float32, least / len(split), largest / len(split))
        return jnp.repeat(jnp.exp(draws), dims[position] // blocks).reshape((-1,) + (1,) * (len(dims) - position - 1))

    level = one(*split[0])
    for cut in split[1:]:
        level = level * one(*cut)
    return level


def shared_out(key, own, number, rows, number_of, top, reach, skew):
    ranking = jax.random.permutation(key, number_of)
    crowded, usual = shares(number_of, rows * top, reach, skew, True), shares(number_of, rows * top, reach, skew, False)
    places = jnp.arange(number_of)

    def named(sizes, turn):
        used = int((sizes > 0).sum())
        fixed = max(1, used // 4)
        moved = fixed + (places - fixed + turn * (used - fixed)) % max(1, number_of - fixed)
        return jnp.zeros((number_of,), jnp.int32).at[ranking[jnp.where(places < fixed, places, moved)]].set(jnp.asarray(sizes, jnp.int32))

    sizes = jnp.where(number % 4 == 0, named(crowded, number // 4), named(usual, number - number // 4 - 1))
    mixed = jax.random.permutation(jax.random.fold_in(own, 3), number_of)
    giver, taker = mixed[0:number_of // 2 * 2:2], mixed[1:number_of // 2 * 2:2]
    room = jnp.minimum(sizes[giver] - 1, reach - sizes[taker]) // 2
    room = jnp.where((giver == ranking[0]) | (taker == ranking[0]) | (sizes[taker] == 0), 0, jnp.maximum(room, 0))
    moved = jax.random.randint(jax.random.fold_in(own, 4), (number_of // 2,), 0, 1 << 20) % (room + 1)
    sizes = sizes.at[giver].add(-moved).at[taker].add(moved)
    items = jnp.searchsorted(jnp.cumsum(sizes), jnp.arange(rows * top), side="right").astype(jnp.int32)
    table = items.reshape(top, rows).T
    table = table[jax.random.permutation(jax.random.fold_in(own, 1), rows)]
    turn = jax.random.randint(jax.random.fold_in(own, 2), (rows, 1), 0, top)
    return jnp.take_along_axis(table, (jnp.arange(top)[None, :] + turn) % top, axis=1)


def shares(count, total, bound, skew, full):
    loads = [(1 << 20) // math.isqrt(rank ** skew) + 1 for rank in range(1, count + 1)]
    largest = bound if full else min(bound, max(-(-total // count), total * loads[0] // sum(loads)))
    least = 1 if total - largest >= count - 1 else 0
    holding, rest = [largest] + [least] * (count - 1), total - largest - least * (count - 1)
    while rest > 0:
        free = [i for i in range(1, count) if holding[i] < largest] or [i for i in range(1, count) if holding[i] < bound]
        mass, remaining = sum([loads[i] for i in free]), rest
        for i in free:
            more = min(bound - holding[i], max(1, remaining * loads[i] // mass), rest)
            holding[i] = holding[i] + more
            rest = rest - more
    return np.array(holding)


def centred(stream_key, dims, spread, limit, shards=(), held_as=jnp.bfloat16):
    entries = spread * jax.random.normal(stream_key, dims, jnp.float32)
    if shards:
        entries = entries * levels(stream_key, dims, shards, -0.22, 0.18)
    return jnp.clip(entries, -limit, limit).astype(held_as)


def setup_inputs(seed: int = 0) -> dict:
    streams_of = jax.random.split(jax.random.key(seed), 16)
    layer_in = centred(streams_of[0], (ITEMS, LENGTH, D), 1.0, 6.0, ((0, 32), (1, 4)))
    w_query = centred(streams_of[1], (D, D), D ** -0.5, 0.1875, ((0, 128),))
    w_key = centred(streams_of[2], (D, D), D ** -0.5, 0.1875, ((0, 128),))
    w_value = centred(streams_of[3], (D, D), D ** -0.5, 0.1875, ((0, 128),))
    w_out = centred(streams_of[4], (D, D), (D // 64) ** -0.5, 1.5, ((0, 128),))
    norm_attn = jnp.clip(1.0 + 0.1 * jax.random.normal(streams_of[5], (D,), jnp.float32), 0.5, 1.5).astype(jnp.bfloat16)
    norm_moe = jnp.clip(1.0 + 0.1 * jax.random.normal(streams_of[6], (D,), jnp.float32), 0.5, 1.5).astype(jnp.bfloat16)
    rel_table = centred(streams_of[7], (BUCKETS * HEADS,), 1.0, 4.0, ((0, 128),))
    w_router = centred(streams_of[8], (D, EXPERTS), (2 * D) ** -0.5, 0.125, ((0, 128),))
    expert_gate = centred(streams_of[9], (EXPERTS, D, FF), D ** -0.5, 0.1875, ((0, 32), (2, 4)))
    expert_up = centred(streams_of[10], (EXPERTS, D, FF), D ** -0.5, 0.1875, ((0, 32), (2, 4)))
    expert_down = centred(streams_of[11], (EXPERTS, FF, D), FF ** -0.5, 0.109375, ((0, 32), (1, 4)))
    routes_keys = jax.random.split(jax.random.fold_in(streams_of[12], 1), ITEMS * LENGTH // SEQ_DEV)
    routes_turns = jax.random.permutation(jax.random.fold_in(streams_of[12], 3), ITEMS * LENGTH // SEQ_DEV)
    routes = jax.vmap(lambda own, number: shared_out(jax.random.fold_in(streams_of[12], 2), own, number, SEQ_DEV, EXPERTS, 2, ROUTE_MOST, 1))(routes_keys, routes_turns).reshape((ITEMS, LENGTH, 2))
    rel_bucket = draw_rel_bucket(jax.random.fold_in(streams_of[15], 71), 0)
    cotangent = centred(streams_of[14], (ITEMS, LENGTH, D), 1.0, 6.0, ((0, 32), (1, 4)))
    return dict(layer_in=layer_in, w_query=w_query, w_key=w_key, w_value=w_value, w_out=w_out, norm_attn=norm_attn, norm_moe=norm_moe, rel_table=rel_table, w_router=w_router, expert_gate=expert_gate, expert_up=expert_up, expert_down=expert_down, routes=routes, rel_bucket=rel_bucket, cotangent=cotangent)


EPSILON = 1e-06
highest = lax.Precision.HIGHEST

@jax.custom_vjp
def low(v):
    return lax.optimization_barrier(v.astype(jnp.bfloat16)).astype(jnp.float32)

@jax.custom_vjp
def low_back(v):
    return v

def low_keep(v):
    return (low(v), None)

def low_pass(kept, grad):
    return (grad,)

def back_keep(v):
    return (v, None)

def back_low(kept, grad):
    return (low(grad),)
low.defvjp(low_keep, low_pass)
low_back.defvjp(back_keep, back_low)

def rms_norm(values, gain):
    return values * lax.rsqrt(lax.optimization_barrier(jnp.mean(values * values, -1, keepdims=True)) + EPSILON) * gain

def attention_items(block, w_query, w_key, w_value, w_out, gain, position_bias):
    count = block.shape[0]
    hidden = low(rms_norm(block, gain))

    def project(weight):
        result = low(low_back(jnp.einsum('nld,de->nle', hidden, weight, precision=highest)))
        return result.reshape(count, LENGTH, HEADS, HEAD_DIM)
    query = project(w_query)
    keys = project(w_key)
    values = project(w_value)
    scores = jnp.einsum('nqhd,nkhd->nhqk', query, keys, precision=highest) * HEAD_DIM ** (-0.5) + position_bias[None]
    scores = low_back(scores)
    probs = jax.nn.softmax(scores, -1)
    mixed = jnp.einsum('nhqk,nkhd->nqhd', low(probs), values, precision=highest)
    mixed = low(low_back(mixed)).reshape(count, LENGTH, D)
    attended = low_back(jnp.einsum('nld,de->nle', mixed, w_out, precision=highest))
    return block + attended

def to_groups(values):
    shaped = values.reshape((N_DP, ITEMS_DP, N_SEQ, SEQ_DEV) + values.shape[2:])
    return jnp.swapaxes(shaped, 1, 2).reshape((N_DP * N_SEQ * TOK_DEV,) + values.shape[2:])

def from_groups(values):
    shaped = values.reshape((N_DP, N_SEQ, ITEMS_DP, SEQ_DEV) + values.shape[1:])
    return jnp.swapaxes(shaped, 1, 2).reshape((ITEMS, LENGTH) + values.shape[1:])

def reference(layer_in, w_query, w_key, w_value, w_out, norm_attn, norm_moe, rel_table, w_router, expert_gate, expert_up, expert_down, routes, rel_bucket, cotangent):
    groups = N_DP * N_SEQ
    total = groups * TOK_DEV
    grouped_routes = to_groups(routes)
    korder = grouped_routes.reshape(groups, TOK_DEV, 2).transpose(0, 2, 1).reshape(groups, 2 * TOK_DEV)
    order_hot = (korder[:, :, None] == jnp.arange(EXPERTS)[None, None, :]).astype(jnp.int32)
    before = jnp.cumsum(order_hot, 1) - order_hot
    slot_order = lax.optimization_barrier(jnp.sum(before * order_hot, -1))
    dropped = lax.optimization_barrier(jnp.sum(order_hot * (slot_order >= CAP)[:, :, None].astype(jnp.int32), (0, 1)))
    counts = jnp.stack([lax.optimization_barrier(jnp.sum(order_hot, (0, 1))), dropped]).astype(jnp.int32)
    slots = slot_order.reshape(groups, 2, TOK_DEV).transpose(0, 2, 1)
    kept = slots < CAP
    group_ids = jnp.arange(groups, dtype=jnp.int32)[:, None, None]
    token_ids = jnp.arange(TOK_DEV, dtype=jnp.int32)[None, :, None]
    choice_ids = jnp.arange(2, dtype=jnp.int32)[None, None, :]
    route_ids = ((group_ids * TOK_DEV + token_ids) * 2 + choice_ids).astype(jnp.int32)
    positions = jnp.where(kept, group_ids * CAP + slots, groups * CAP).astype(jnp.int32)
    table_ids = jnp.full((EXPERTS, groups * CAP), 2 * total, jnp.int32)
    table_ids = table_ids.at[grouped_routes.reshape(groups, TOK_DEV, 2).reshape(-1), positions.reshape(-1)].set(route_ids.reshape(-1), mode='drop')
    flat_routes = grouped_routes.reshape(total, 2)
    offsets = jnp.arange(LENGTH, dtype=jnp.int32)[None, :] - jnp.arange(LENGTH, dtype=jnp.int32)[:, None] + (LENGTH - 1)
    bucket_hot = (rel_bucket[offsets][:, :, None] == jnp.arange(BUCKETS, dtype=jnp.int32)[None, None, :]).astype(jnp.float32)
    per_group = math.gcd(ITEMS, max(1, 4096 // LENGTH))

    def forward(inputs, wq, wk, wv, wo, gain_attn, gain_moe, table_flat, router, gate_all, up_all, down_all):
        table = table_flat.reshape(BUCKETS, HEADS)
        position_bias = jnp.einsum('qkb,bh->hqk', bucket_hot, table, precision=highest)
        blocks = inputs.reshape(ITEMS // per_group, per_group, LENGTH, D)
        step = jax.checkpoint(lambda block: attention_items(block, wq, wk, wv, wo, gain_attn, position_bias))
        resid = lax.map(step, blocks).reshape(ITEMS, LENGTH, D)
        hidden = low(rms_norm(resid, gain_moe))
        grouped = to_groups(hidden)
        logits = low_back(jnp.dot(grouped, router, precision=highest))
        chosen = jnp.take_along_axis(logits, flat_routes, 1)
        gates = jax.nn.softmax(chosen, -1)
        gate_flat = jnp.concatenate([gates.reshape(-1), jnp.zeros((1,), jnp.float32)])
        padded = jnp.concatenate([grouped, jnp.zeros((1, D), jnp.float32)], 0)

        def expert_step(pieces):
            gate_w, up_w, down_w, ids = pieces
            rows = low_back(padded[ids // 2])
            gate_pre = low_back(jnp.dot(rows, gate_w, precision=highest))
            up_pre = low_back(jnp.dot(rows, up_w, precision=highest))
            active = low(jax.nn.gelu(gate_pre) * up_pre)
            return low(low_back(jnp.dot(active, down_w, precision=highest)))
        outputs = lax.map(jax.checkpoint(expert_step), (gate_all, up_all, down_all, table_ids))
        weights = gate_flat[table_ids]
        mixture = jnp.zeros((total + 1, D), jnp.float32)
        mixture = mixture.at[(table_ids // 2).reshape(-1)].add((weights[:, :, None] * outputs).reshape(-1, D))
        return resid + from_groups(mixture[:total])
    primal_in = (layer_in.astype(jnp.float32), w_query.astype(jnp.float32), w_key.astype(jnp.float32), w_value.astype(jnp.float32), w_out.astype(jnp.float32), norm_attn.astype(jnp.float32), norm_moe.astype(jnp.float32), rel_table.astype(jnp.float32), w_router.astype(jnp.float32), expert_gate.astype(jnp.float32), expert_up.astype(jnp.float32), expert_down.astype(jnp.float32))
    result, pullback = jax.vjp(forward, *primal_in)
    grads = pullback(cotangent.astype(jnp.float32))
    return (result.astype(jnp.bfloat16), grads[0], grads[1], grads[2], grads[3], grads[4], grads[5], grads[6], grads[7], grads[8], grads[9], grads[10], grads[11], counts)
```

```python
import math

import jax
import jax.numpy as jnp
from jax import lax
from jax.experimental import pallas as pl
from jax.experimental.pallas import tpu as pltpu
from jax.sharding import PartitionSpec as P

MESH = pl.DeviceIdType.MESH
ANY = pl.BlockSpec(memory_space=pl.ANY)
VMEM = pl.BlockSpec(memory_space=pltpu.VMEM)
DMA = pltpu.SemaphoreType.DMA
F32 = jnp.float32
BF16 = jnp.bfloat16

D = 1024
HEADS = 16
SIZE = 64
BUCKETS = 32
EXPERTS = 32
LENGTH = 512
ROWS = 128
CAP = 20
MAIN = 16
EPSILON = 1e-06

SLAB = 4 * 1024 + 256
PARTS = ((0, 1536), (1536, 1408), (2944, 1408))
ORDERS = ("xyz", "yzx", "zxy")
TAIL = 256 + 128
GRAD = 3 * 256 + 128 + 256
THIRD = GRAD // 3


def div(a, b):
    return lax.div(a, jnp.int32(b))


def rem(a, b):
    return lax.rem(a, jnp.int32(b))


def place():
    dp, seq = lax.axis_index("dp"), lax.axis_index("seq")
    x = div(seq, 2) * 2 + rem(div(dp, 4), 2)
    return x, div(dp, 8), rem(dp, 4), rem(seq, 2)


def device(x, y, z, core):
    return ((y * 2 + rem(x, 2)) * 4 + z, div(x, 2) * 2 + core)


def greet(devices):
    barrier = pltpu.get_barrier_semaphore()
    for one in devices:
        pl.semaphore_signal(barrier, inc=1, device_id=one, device_id_type=MESH)
    pl.semaphore_wait(barrier, len(devices))


def remote(src, dst, send, recv, to):
    return pltpu.make_async_remote_copy(
        src_ref=src, dst_ref=dst, send_sem=send, recv_sem=recv, device_id=to, device_id_type=MESH
    )


def params(collective, megabytes):
    return pltpu.CompilerParams(
        collective_id=collective, has_side_effects=True, vmem_limit_bytes=megabytes << 20
    )


def cost(sent, flops=0):
    return pl.CostEstimate(flops=flops, bytes_accessed=sent, transcendentals=0)


def seq_gather_start(own, full, relay, sems):
    local, send, recv = sems
    x, y, z, core = place()
    right, left = device(rem(x + 1, 4), y, z, core), device(rem(x + 3, 4), y, z, core)
    sibling = device(x, y, z, 1 - core)
    me = div(x, 2) * 2 + core
    mine = pltpu.make_async_copy(own, full.at[:, me], local)
    copies = [
        remote(own, full.at[:, me], send.at[0], recv.at[0], sibling),
        remote(own.at[0], relay.at[0], send.at[1], recv.at[1], right),
        remote(own.at[1], relay.at[1], send.at[2], recv.at[2], left),
    ]
    mine.start()
    for copy in copies[1:] + copies[:1]:
        copy.start()
    return mine, copies


def seq_gather_finish(state, full, relay, sems):
    local, send, recv = sems
    mine, copies = state
    x, y, z, core = place()
    right, left = device(rem(x + 1, 4), y, z, core), device(rem(x + 3, 4), y, z, core)
    sibling = device(x, y, z, 1 - core)
    from_left = div(rem(x + 3, 4), 2) * 2 + core
    from_right = div(rem(x + 1, 4), 2) * 2 + core
    partner = rem(div(x, 2) + 1, 2) * 2 + core
    onward = [
        remote(relay.at[0], full.at[0, from_left], send.at[3], recv.at[3], right),
        remote(relay.at[1], full.at[1, from_right], send.at[4], recv.at[4], left),
    ]
    across = [
        remote(full.at[0, partner], full.at[0, partner], send.at[5], recv.at[5], sibling),
        remote(full.at[1, partner], full.at[1, partner], send.at[6], recv.at[6], sibling),
    ]
    for item in range(2):
        copies[1 + item].wait_recv()
        onward[item].start()
    for item in range(2):
        onward[item].wait_recv()
        across[item].start()
    mine.wait()
    copies[0].wait_recv()
    for copy in across:
        copy.wait_recv()
    for copy in copies + onward + across:
        copy.wait_send()


def chips(k):
    x, y, z, core = place()
    kx, ky, kz = div(k, 16), rem(div(k, 4), 4), rem(k, 4)
    ahead = (rem(x + kx, 4), rem(y + ky, 4), rem(z + kz, 4))
    behind = (rem(x + 4 - kx, 4), rem(y + 4 - ky, 4), rem(z + 4 - kz, 4))
    return ahead, behind


def greet_chips():
    x, y, z, core = place()
    barrier = pltpu.get_barrier_semaphore()

    @pl.loop(1, 64)
    def _(k):
        ahead, _ = chips(k)
        pl.semaphore_signal(barrier, inc=1, device_id=device(*ahead, core), device_id_type=MESH)

    pl.semaphore_signal(barrier, inc=1, device_id=device(x, y, z, 1 - core), device_id_type=MESH)
    pl.semaphore_wait(barrier, 64)


def peers(k):
    x, y, z, core = place()
    kx, ky, kz = div(k, 16), rem(div(k, 4), 4), rem(k, 4)
    return device(div(x, 2) * 2 + rem(rem(x, 2) + kx, 2), rem(y + ky, 4), rem(z + kz, 4), core)


def greet_peers(others):
    barrier = pltpu.get_barrier_semaphore()

    @pl.loop(1, 32)
    def _(k):
        pl.semaphore_signal(barrier, inc=1, device_id=peers(k), device_id_type=MESH)

    for one in others:
        pl.semaphore_signal(barrier, inc=1, device_id=one, device_id_type=MESH)
    pl.semaphore_wait(barrier, 31 + len(others))


class Exchange:
    def __init__(self, slabs, rows, local, send, recv):
        self.slabs, self.rows = slabs, rows
        self.local, self.send, self.recv = local, send, recv
        self.dp = lax.axis_index("dp")

    def packet(self, k):
        to = peers(k)
        return [
            remote(slab.at[to[0]], rows.at[self.dp], self.send.at[i, k], self.recv.at[i, k], to)
            for i, (slab, rows) in enumerate(zip(self.slabs, self.rows))
        ]

    def kept(self):
        return [
            pltpu.make_async_copy(slab.at[self.dp], rows.at[self.dp], self.local.at[i])
            for i, (slab, rows) in enumerate(zip(self.slabs, self.rows))
        ]

    def start(self, first, last):
        @pl.loop(first, last)
        def _(k):
            for copy in self.packet(k):
                copy.start()

    def keep(self):
        for copy in self.kept():
            copy.start()

    def finish(self):
        @pl.loop(1, 32)
        def _(k):
            for copy in self.packet(k):
                copy.wait_recv()
                copy.wait_send()

        for copy in self.kept():
            copy.wait()


EXCHANGE_SEMS = [DMA((2,)), DMA((2, 32)), DMA((2, 32))]


def gather_kernel(
    slab,
    own,
    main,
    extra,
    full,
    items,
    mains,
    extras,
    relay,
    local,
    send,
    recv,
    near_send,
    near_recv,
    seq_local,
    seq_send,
    seq_recv,
    *exchange_sems,
):
    x, y, z, core = place()
    at = {"x": x, "y": y, "z": z}
    sibling = device(x, y, z, 1 - core)

    def moved(axis, by):
        return dict(at, **{axis: rem(at[axis] + by, 4)})

    def who(spot):
        return device(spot["x"], spot["y"], spot["z"], core)

    greet_peers([who(moved(axis, by)) for axis in "xyz" for by in (1, 3)] + [sibling])
    packets = Exchange((main, extra), (mains, extras), *exchange_sems)

    def block(spot, whole, first, width):
        every = slice(None)
        row = every if "y" in whole else spot["y"]
        depth = every if "z" in whole else spot["z"]
        near, far = every, every
        if "x" not in whole:
            near, far = rem(spot["x"], 2), div(spot["x"], 2)
        return full.at[row, near, depth, far, core, :, pl.ds(first, width)]

    near = []

    def share(ref):
        k = len(near)
        copy = remote(ref, ref, near_send.at[k], near_recv.at[k], sibling)
        copy.start()
        near.append(copy)

    own_place = full.at[y, rem(x, 2), z, div(x, 2), core]
    mine = pltpu.make_async_copy(slab, own_place, local)
    mine.start()
    sems = (seq_local, seq_send, seq_recv)
    state = seq_gather_start(own, items, relay, sems)
    packets.keep()
    mine.wait()
    share(own_place)
    sent = []
    for stage in range(3):
        steps = []
        for part in range(3):
            axis, whole = ORDERS[part][stage], ORDERS[part][:stage]
            first, width = PARTS[part]
            near_half = 768
            k = (part * 3 + stage) * 4
            right, left = who(moved(axis, 1)), who(moved(axis, 3))
            here = block(at, whole, first, width)
            there_left, there_right = moved(axis, 3), moved(axis, 1)
            part_left = block(there_left, whole, first, near_half)
            part_right = block(there_right, whole, first + near_half, width - near_half)
            copies = [
                remote(here, here, send.at[k], recv.at[k], right),
                remote(here, here, send.at[k + 1], recv.at[k + 1], left),
                remote(part_left, part_left, send.at[k + 2], recv.at[k + 2], right),
                remote(part_right, part_right, send.at[k + 3], recv.at[k + 3], left),
            ]
            copies[0].start()
            copies[1].start()
            opposite = moved(axis, 2)
            steps.append(
                (
                    copies,
                    [
                        block(there_left, whole, first, width),
                        block(there_right, whole, first, width),
                        block(opposite, whole, first, near_half),
                        block(opposite, whole, first + near_half, width - near_half),
                    ],
                )
            )
            sent.extend(copies)
        packets.start(*((1, 11), (11, 22), (22, 32))[stage])
        for copies, arrived in steps:
            for k in range(2):
                copies[k].wait_recv()
                copies[k + 2].start()
                share(arrived[k])
        for copies, arrived in steps:
            for k in range(2, 4):
                copies[k].wait_recv()
                share(arrived[k])
    seq_gather_finish(state, items, relay, sems)
    packets.finish()
    for copy in near:
        copy.wait_recv()
    for copy in sent + near:
        copy.wait_send()


def gather_all(slab, own, main, extra):
    return pl.pallas_call(
        gather_kernel,
        out_shape=(
            jax.ShapeDtypeStruct((4, 2, 4, 2, 2, 8, SLAB), BF16),
            jax.ShapeDtypeStruct((2, 4, 16, 8, D), BF16),
            jax.ShapeDtypeStruct((32, 2, 8, D), BF16),
            jax.ShapeDtypeStruct((32, 2, 8, 256), BF16),
        ),
        in_specs=[ANY] * 4,
        out_specs=(ANY,) * 4,
        scratch_shapes=[
            pltpu.VMEM((2, 16, 8, D), BF16),
            DMA(()),
            DMA((36,)),
            DMA((36,)),
            DMA((37,)),
            DMA((37,)),
            DMA(()),
            DMA((7,)),
            DMA((7,)),
            *EXCHANGE_SEMS,
        ],
        compiler_params=params(0, 32),
        cost_estimate=cost(90 << 20),
    )(slab, own, main, extra)


def items_kernel(own, full, relay, local, send, recv):
    x, y, z, core = place()
    greet(
        [
            device(rem(x + 1, 4), y, z, core),
            device(rem(x + 3, 4), y, z, core),
            device(x, y, z, 1 - core),
        ]
    )
    sems = (local, send, recv)
    state = seq_gather_start(own, full, relay, sems)
    seq_gather_finish(state, full, relay, sems)


def gather_items(own):
    return pl.pallas_call(
        items_kernel,
        out_shape=jax.ShapeDtypeStruct((2, 4, 16, 8, D), BF16),
        in_specs=[ANY],
        out_specs=ANY,
        scratch_shapes=[pltpu.VMEM((2, 16, 8, D), BF16), DMA(()), DMA((7,)), DMA((7,))],
        compiler_params=params(1, 32),
        cost_estimate=cost(20 << 20),
    )(own)


def grads_kernel(
    heads,
    rest,
    part,
    main,
    extra,
    mine,
    other,
    small,
    wide,
    mains,
    extras,
    own,
    got,
    relay,
    first_in,
    first_sum,
    second_in,
    total,
    own_local,
    near_send,
    near_recv,
    relay_send,
    relay_recv,
    first_local,
    first_send,
    first_recv,
    second_send,
    second_recv,
    last_local,
    last_send,
    last_recv,
    *exchange_sems,
):
    x, y, z, core = place()
    my_dp, my_seq = device(x, y, z, core)
    sibling = device(x, y, z, 1 - core)
    right, left = device(rem(x + 1, 4), y, z, core), device(rem(x + 3, 4), y, z, core)
    here = div(x, 2)
    away = 1 - here

    greet_peers([(my_dp, rem(my_seq + step, 4)) for step in range(1, 4)] + [right, left])

    shares = []
    for k, side in enumerate((away, here)):
        shares.append(
            (
                remote(
                    part.at[:, side * 2 + 1 - core],
                    got.at[k],
                    near_send.at[k],
                    near_recv.at[k],
                    sibling,
                ),
                pltpu.make_async_copy(part.at[:, side * 2 + core], own.at[k], own_local.at[k]),
            )
        )
        for copy in shares[k]:
            copy.start()

    near, every = rem(x, 2), slice(None)
    sizes = (4, 4, 2)
    low, high = pl.ds(0, THIRD), pl.ds(THIRD, THIRD)

    def piece(index, step):
        if index == 0:
            return heads.at[rem(y + step, 4), :, :, :, :, low]
        if index == 1:
            return heads.at[:, :, rem(z + step, 4), :, :, high]
        return rest.at[:, rem(near + step, 2)]

    def along(index, step):
        if index == 0:
            return device(x, rem(y + step, 4), z, core)
        if index == 1:
            return device(x, y, rem(z + step, 4), core)
        return device(here * 2 + rem(near + step, 2), y, z, core)

    firsts, keeps = [], []
    for index in range(3):
        for step in range(sizes[index]):
            k = index * 4 + step
            if step == 0:
                copy = pltpu.make_async_copy(
                    piece(index, 0), first_in[index].at[0], first_local.at[index]
                )
                keeps.append(copy)
            else:
                copy = remote(
                    piece(index, step),
                    first_in[index].at[step],
                    first_send.at[k],
                    first_recv.at[k],
                    along(index, step),
                )
                firsts.append((index, copy))
            copy.start()
    packets = Exchange((main, extra), (mains, extras), *exchange_sems)
    packets.start(1, 32)
    packets.keep()

    shares[0][1].wait()
    shares[0][0].wait_recv()
    hops = [
        remote(own.at[0, 0], relay.at[0], relay_send.at[0], relay_recv.at[0], right),
        remote(own.at[0, 1], relay.at[1], relay_send.at[1], relay_recv.at[1], left),
        remote(relay.at[0], other.at[0], relay_send.at[2], relay_recv.at[2], right),
        remote(relay.at[1], other.at[1], relay_send.at[3], relay_recv.at[3], left),
    ]
    for item in range(2):

        @pl.loop(0, 8)
        def _(row):
            rows = pl.ds(row * 2, 2)
            summed = own[0, item, rows].astype(F32) + got[0, item, rows].astype(F32)
            own[0, item, rows] = summed.astype(BF16)

        hops[item].start()
    shares[1][1].wait()
    shares[1][0].wait_recv()
    for item in range(2):

        @pl.loop(0, 8)
        def _(row):
            rows = pl.ds(row * 2, 2)
            mine[item, rows] = own[1, item, rows].astype(F32) + got[1, item, rows].astype(F32)

    for item in range(2):
        hops[item].wait_recv()
        hops[2 + item].start()

    def to_second(index, k):
        if index == 0:
            a, b = rem(near + div(k, 4), 2), rem(z + rem(k, 4), 4)
            return (a, b), device(here * 2 + a, y, b, core)
        if index == 1:
            a, b = rem(y + rem(k, 4), 4), rem(near + div(k, 4), 2)
            return (a, b), device(here * 2 + b, a, z, core)
        a, b = rem(y + div(k, 4), 4), rem(z + rem(k, 4), 4)
        return (a, b), device(x, a, b, core)

    def second(index, k):
        spot, to = to_second(index, k)
        slot = index * 8 + k
        return remote(
            first_sum[index].at[spot],
            second_in.at[slot],
            second_send.at[slot],
            second_recv.at[slot],
            to,
        )

    counts = (8, 8, 16)
    for index in range(3):
        keeps[index].wait()
        for which, copy in firsts:
            if which == index:
                copy.wait_recv()
        held, summed = first_in[index], first_sum[index]
        rows, columns = summed.shape[0], summed.shape[1]

        @pl.loop(0, rows)
        def _(a):
            for b in range(columns):
                value = held[0, a, b].astype(F32)
                for step in range(1, sizes[index]):
                    value = value + held[step, a, b].astype(F32)
                summed[a, b] = value.astype(BF16)

        @pl.loop(1, counts[index])
        def _(k):
            second(index, k).start()

    for index in range(3):
        columns = pl.ds(index * THIRD, THIRD)
        total[:, :, columns] = first_sum[index][to_second(index, jnp.int32(0))[0]].astype(F32)

        @pl.loop(1, counts[index])
        def _(k):
            second(index, k).wait_recv()
            total[:, :, columns] += second_in[index * 8 + k].astype(F32)

    columns = 3 * 256 + 128
    last = []
    for step in range(1, 4):
        seq = rem(my_seq + step, 4)
        copy = remote(
            total.at[seq, :, pl.ds(0, columns)],
            small.at[my_seq],
            last_send.at[step],
            last_recv.at[step],
            (my_dp, seq),
        )
        copy.start()
        last.append(copy)
    keep = pltpu.make_async_copy(
        total.at[my_seq, :, pl.ds(0, columns)],
        small.at[my_seq],
        last_local,
    )
    keep.start()
    wide[...] = total[:, :, columns:]
    keep.wait()
    for copy in last:
        copy.wait_recv()
    for item in range(2):
        hops[2 + item].wait_recv()
    packets.finish()
    for copy in last + hops + [share[0] for share in shares]:
        copy.wait_send()

    for _, copy in firsts:
        copy.wait_send()
    for index in range(3):

        @pl.loop(1, counts[index])
        def _(k):
            second(index, k).wait_send()


def reduce_grads(heads, rest, part, main, extra):
    columns = 3 * 256 + 128
    return pl.pallas_call(
        grads_kernel,
        out_shape=(
            jax.ShapeDtypeStruct((2, 16, 8, D), F32),
            jax.ShapeDtypeStruct((2, 16, 8, D), BF16),
            jax.ShapeDtypeStruct((4, 8, columns), F32),
            jax.ShapeDtypeStruct((4, 8, 256), F32),
            jax.ShapeDtypeStruct((32, 2, 8, D), BF16),
            jax.ShapeDtypeStruct((32, 2, 8, 256), BF16),
        ),
        in_specs=[ANY] * 5,
        out_specs=(VMEM, ANY, VMEM, VMEM, ANY, ANY),
        scratch_shapes=[
            pltpu.VMEM((2, 2, 16, 8, D), BF16),
            pltpu.VMEM((2, 2, 16, 8, D), BF16),
            pltpu.VMEM((2, 16, 8, D), BF16),
            [
                pltpu.VMEM((4, 2, 4, 4, 8, THIRD), BF16),
                pltpu.VMEM((4, 4, 2, 4, 8, THIRD), BF16),
                pltpu.VMEM((2, 4, 4, 4, 8, THIRD), BF16),
            ],
            [
                pltpu.VMEM((2, 4, 4, 8, THIRD), BF16),
                pltpu.VMEM((4, 2, 4, 8, THIRD), BF16),
                pltpu.VMEM((4, 4, 4, 8, THIRD), BF16),
            ],
            pltpu.VMEM((32, 4, 8, THIRD), BF16),
            pltpu.VMEM((4, 8, GRAD), F32),
            DMA((2,)),
            DMA((2,)),
            DMA((2,)),
            DMA((4,)),
            DMA((4,)),
            DMA((3,)),
            DMA((12,)),
            DMA((12,)),
            DMA((32,)),
            DMA((32,)),
            DMA(()),
            DMA((4,)),
            DMA((4,)),
            *EXCHANGE_SEMS,
        ],
        compiler_params=params(4, 48),
        cost_estimate=cost(60 << 20),
    )(heads, rest, part, main, extra)


NT = (((1,), (1,)), ((), ()))
TN = (((0,), (0,)), ((), ()))


def dot(a, b, dims=None):
    if dims is None:
        return jnp.dot(a, b, preferred_element_type=F32)
    return lax.dot_general(a, b, dims, preferred_element_type=F32)


def bias_rows(window):
    return pltpu.roll(
        jnp.broadcast_to(window, (ROWS, 640)), 640 - 127, 1, stride=1, stride_axis=0
    )[:, :LENGTH]


def flat(rows):
    return rows.astype(F32).reshape(rows.shape[0] * 8, 128).astype(BF16)


def tiled(rows):
    return rows.reshape(rows.shape[0] // 8, 8, 128).astype(BF16)


def softmax(scores):
    powers = jnp.exp(scores - jnp.max(scores, -1, keepdims=True))
    return powers * (1.0 / jnp.sum(powers, -1, keepdims=True))


def forward_kernel(window, query, key, value, mixed):
    low = lax.broadcasted_iota(jnp.int32, (ROWS, 128), 1) < SIZE
    biases = [bias_rows(window[0, head : head + 1]) for head in range(2)]
    for item in range(2):
        queries = query[item].astype(F32).reshape(ROWS, 128) * SIZE**-0.5
        keys, values = flat(key[item]), flat(value[item])
        results = []
        for head in range(2):
            own = low if head == 0 else ~low
            one = jnp.where(own, queries, 0.0).astype(BF16)
            scores = dot(one, keys, NT) + biases[head]
            results.append(dot(softmax(scores).astype(BF16), values))
        mixed[item] = tiled(jnp.where(low, results[0], results[1]))


def attend(windows, query, key_value):
    def block(rows, first=0):
        return pl.BlockSpec((2, rows // 8, 8, 128), lambda pair: (0, 0, 0, first + pair))

    return pl.pallas_call(
        forward_kernel,
        grid=(HEADS // 2,),
        out_shape=jax.ShapeDtypeStruct((2, ROWS // 8, 8, D), BF16),
        in_specs=[
            pl.BlockSpec((1, 2, 640), lambda pair: (pair, 0, 0)),
            block(ROWS),
            block(LENGTH),
            block(LENGTH, HEADS // 2),
        ],
        out_specs=block(ROWS),
        compiler_params=pltpu.CompilerParams(vmem_limit_bytes=32 << 20),
        cost_estimate=cost(12 << 20, 4 << 30),
    )(windows, query, key_value, key_value)


def backward_kernel(windows, query, key, value, grad, mixed, dquery, dkey, dvalue, dbias):
    low = lax.broadcasted_iota(jnp.int32, (LENGTH, 128), 1) < SIZE
    keys, values = flat(key[0]), flat(value[0])
    all_queries = query[0].astype(F32).reshape(LENGTH, 128) * SIZE**-0.5
    all_grads = grad[0].astype(F32).reshape(LENGTH, 128)
    blocks = LENGTH // ROWS
    results = []
    for head in range(2):
        own = low if head == 0 else ~low
        queries = jnp.where(own, all_queries, 0.0).astype(BF16)
        grads = jnp.where(own, all_grads, 0.0).astype(BF16)
        bias = jnp.concatenate(
            [bias_rows(windows[0, head, block : block + 1]) for block in range(blocks)], 0
        )
        probs = softmax(dot(queries, keys, NT) + bias)
        low_probs = probs.astype(BF16)
        dprobs = dot(grads, values, NT)
        dscores = probs * (dprobs - jnp.sum(probs * dprobs, -1, keepdims=True))
        low_scores = dscores.astype(BF16)
        results.append(
            (
                dot(low_probs, values),
                dot(low_scores, keys) * SIZE**-0.5,
                dot(low_scores, queries, TN),
                dot(low_probs, grads, TN),
            )
        )
        diagonal = jnp.zeros((1, 1024), F32)
        for block in range(blocks):
            sums = jnp.concatenate(
                [
                    low_scores[block * ROWS : block * ROWS + ROWS].astype(F32),
                    jnp.zeros((ROWS, 128), F32),
                ],
                axis=1,
            )
            count = ROWS
            while count > 1:
                count //= 2
                sums = pltpu.roll(sums[:count], count, 1) + sums[count:]
            first = LENGTH - ROWS - block * ROWS
            pieces = [sums]
            if first:
                pieces.insert(0, jnp.zeros((1, first), F32))
            if first + 640 < 1024:
                pieces.append(jnp.zeros((1, 1024 - 640 - first), F32))
            diagonal = diagonal + jnp.concatenate(pieces, axis=1)
        dbias[0, 0, head : head + 1] = diagonal
    for ref, one, two in zip((mixed, dquery, dkey, dvalue), *results):
        ref[0] = tiled(jnp.where(low, one, two))


def attend_back(windows, query, key, value, grad):
    block = pl.BlockSpec((1, LENGTH // 8, 8, 128), lambda pair, item: (item, 0, 0, pair))
    shape = jax.ShapeDtypeStruct((2, LENGTH // 8, 8, 256), BF16)
    return pl.pallas_call(
        backward_kernel,
        grid=(2, 2),
        out_shape=(shape,) * 4 + (jax.ShapeDtypeStruct((2, 2, 2, 1024), F32),),
        in_specs=[
            pl.BlockSpec((1, 2, 4, 640), lambda pair, item: (pair, 0, 0, 0)),
            block,
            block,
            block,
            block,
        ],
        out_specs=(block,) * 4
        + (pl.BlockSpec((1, 1, 2, 1024), lambda pair, item: (item, pair, 0, 0)),),
        compiler_params=pltpu.CompilerParams(vmem_limit_bytes=48 << 20),
        cost_estimate=cost(12 << 20, 8 << 30),
    )(windows, query, key, value, grad)


def rows_of(packets):
    count, width = packets.shape[0], packets.shape[-1]
    return packets.astype(F32).reshape(count * 16, width).astype(BF16)


def packets_of(rows):
    return rows.astype(F32).reshape(rows.shape[0] // 16, 2, 8, rows.shape[1]).astype(BF16)


def expert_rows(rows, grads, gates, gate_w, up_w, down_w, dgate, dup, ddown):
    gate_pre = dot(rows, gate_w[...], NT)
    up_pre = dot(rows, up_w[...], NT)
    square = gate_pre * gate_pre
    root = math.sqrt(2 / math.pi)
    tanh = jnp.tanh(root * gate_pre * (1.0 + 0.044715 * square))
    half = 0.5 * (1.0 + tanh)
    value = gate_pre * half
    slope = half + (0.5 * root) * gate_pre * (1.0 - tanh * tanh) * (1.0 + 3 * 0.044715 * square)
    active = (value * up_pre).astype(BF16)
    out = dot(active, down_w[...])
    grads = grads.astype(F32)
    grad_gates = jnp.sum(out * grads, -1, keepdims=True)
    grad_out = (gates * grads).astype(BF16)
    grad_active = dot(grad_out, down_w[...], NT)
    grad_gate = (grad_active * up_pre * slope).astype(BF16)
    grad_up = (grad_active * value).astype(BF16)
    grad_rows = dot(grad_gate, gate_w[...]) + dot(grad_up, up_w[...])
    dgate[...] += dot(grad_gate, rows, TN)
    dup[...] += dot(grad_up, rows, TN)
    ddown[...] += dot(active, grad_out, TN)
    return out.astype(BF16), grad_rows.astype(BF16), grad_gates


def moe_kernel(
    main,
    tail,
    grads_main,
    grads_extra,
    gate_w,
    up_w,
    down_w,
    back_main,
    back_tail,
    out_main,
    out_extra,
    dgate,
    dup,
    ddown,
    own_main,
    own_tail,
    sib_main,
    sib_tail,
    grad_main,
    grad_extra,
    res_main,
    res_extra,
    part_main,
    part_tail,
    give_main,
    give_tail,
    got_main,
    got_tail,
    keep_sem,
    send,
    recv,
    near_send,
    near_recv,
    grad_sem,
    res_sem,
    give_send,
    give_recv,
    back_keep,
    back_send,
    back_recv,
):
    x, y, z, core = place()
    my_dp = device(x, y, z, core)[0]
    sibling = device(x, y, z, 1 - core)
    greet_chips()
    slabs, own, sib = (main, tail), (own_main, own_tail), (sib_main, sib_tail)
    part, give, got = (part_main, part_tail), (give_main, give_tail), (got_main, got_tail)
    back = (back_main, back_tail)
    per = 8

    def packet(k):
        to = device(*chips(k)[0], core)
        return [
            remote(slabs[i].at[to[0]], own[i].at[k], send.at[i, k], recv.at[i, k], to)
            for i in range(2)
        ]

    def keep():
        return [
            pltpu.make_async_copy(slabs[i].at[my_dp], own[i].at[0], keep_sem.at[i])
            for i in range(2)
        ]

    def share(k):
        return [
            remote(own[i].at[k], sib[i].at[k], near_send.at[i, k], near_recv.at[i, k], sibling)
            for i in range(2)
        ]

    def arrive(block):
        @pl.loop(0, per)
        def _(j):
            k = block * per + j

            @pl.when(k > 0)
            def _():
                for copy in packet(k):
                    copy.wait_recv()

            for copy in share(k):
                copy.start()

    def fetches(block, j):
        slot = rem(block, 2)
        copies = []
        for side in range(2):
            dp, seq = device(*chips(block * per + j)[1], core if side == 0 else 1 - core)
            for i, (source, held) in enumerate(((grads_main, grad_main), (grads_extra, grad_extra))):
                place_at = side * per + j
                copies.append(
                    pltpu.make_async_copy(
                        source.at[seq, dp], held.at[slot, place_at], grad_sem.at[i, slot, place_at]
                    )
                )
        return copies

    def results(block, j):
        slot = rem(block, 2)
        copies = []
        for side in range(2):
            dp, seq = device(*chips(block * per + j)[1], core if side == 0 else 1 - core)
            for i, (held, target) in enumerate(((res_main, out_main), (res_extra, out_extra))):
                place_at = side * per + j
                copies.append(
                    pltpu.make_async_copy(
                        held.at[slot, place_at], target.at[seq, dp], res_sem.at[i, slot, place_at]
                    )
                )
        return copies

    def each(copies, block, act):
        @pl.loop(0, per)
        def _(j):
            for copy in copies(block, j):
                act(copy)

    def hand(block):
        some = pl.ds(block * per, per)
        return [
            remote(
                give[i].at[some],
                got[i].at[some],
                give_send.at[i, block],
                give_recv.at[i, block],
                sibling,
            )
            for i in range(2)
        ]

    def reply(k):
        to = device(*chips(k)[1], core)
        return [
            remote(
                part[i].at[k], back[i].at[div(x, 2), my_dp], back_send.at[i, k], back_recv.at[i, k], to
            )
            for i in range(2)
        ]

    def keep_back():
        return [
            pltpu.make_async_copy(
                part[i].at[0], back[i].at[div(x, 2), my_dp], back_keep.at[i]
            )
            for i in range(2)
        ]

    def finish(block):
        for copy in hand(block):
            copy.wait_recv()

        @pl.loop(0, per)
        def _(j):
            k = block * per + j
            for i in range(2):
                part[i][k] = (part[i][k].astype(F32) + got[i][k].astype(F32)).astype(BF16)

            @pl.when(k > 0)
            def _():
                for copy in reply(k):
                    copy.start()

            @pl.when(k == 0)
            def _():
                for copy in keep_back():
                    copy.start()

    def work(block):
        slot = rem(block, 2)
        some = pl.ds(block * per, per)
        target = lax.broadcasted_iota(jnp.int32, (64, 256), 0)
        source = lax.broadcasted_iota(jnp.int32, (64, 256), 1)
        picks = [(source == 4 * target + m).astype(F32).astype(BF16) for m in range(4)]

        def whole(extra):
            return jnp.concatenate([dot(pick, extra).astype(BF16) for pick in picks], 1)

        def quarters(rows):
            pieces = [
                dot(picks[m], rows[:, 256 * m : 256 * m + 256], TN) for m in range(4)
            ]
            return pieces[0] + pieces[1] + pieces[2] + pieces[3]

        tails = jnp.concatenate([rows_of(own_tail[some]), rows_of(sib_tail[some])], 0)
        rows = jnp.concatenate(
            [rows_of(own_main[some]), rows_of(sib_main[some]), whole(tails[:, :256])], 0
        )
        grads = jnp.concatenate(
            [rows_of(grad_main[slot]), whole(rows_of(grad_extra[slot]))], 0
        )
        scalars = jnp.concatenate([tails[:, 256:].astype(F32), dot(picks[0], tails[:, 256:])], 0)
        first = lax.broadcasted_iota(jnp.int32, (320, 1), 0) < 256
        gates = jnp.where(
            first,
            scalars[:, 0:1] + scalars[:, 1:2],
            scalars[:, 2:3] + scalars[:, 3:4],
        )
        out, grad_rows, grad_gates = expert_rows(
            rows, grads, gates, gate_w, up_w, down_w, dgate, dup, ddown
        )
        res_main[slot] = packets_of(out[:256])
        res_extra[slot] = packets_of(quarters(out[256:]))
        lane = lax.broadcasted_iota(jnp.int32, (320, 128), 1)
        lanes = jnp.where(lane == jnp.where(first, 0, 1), grad_gates, 0.0)
        extra_lanes = lanes[256:].astype(BF16)
        aux = lanes[:256] + (
            dot(picks[0], extra_lanes, TN)
            + dot(picks[1], extra_lanes, TN)
            + dot(picks[2], extra_lanes, TN)
            + dot(picks[3], extra_lanes, TN)
        )
        ends = jnp.concatenate([quarters(grad_rows[256:]), aux], 1)
        part_main[some] = packets_of(grad_rows[:128])
        give_main[some] = packets_of(grad_rows[128:256])
        part_tail[some] = packets_of(ends[:128])
        give_tail[some] = packets_of(ends[128:])

    for copy in keep():
        copy.start()

    @pl.loop(1, 64)
    def _(k):
        for copy in packet(k):
            copy.start()

    each(fetches, 0, lambda copy: copy.start())
    dgate[...] = jnp.zeros_like(dgate)
    dup[...] = jnp.zeros_like(dup)
    ddown[...] = jnp.zeros_like(ddown)
    for copy in keep():
        copy.wait()
    arrive(0)
    blocks = 64 // per

    @pl.loop(0, blocks)
    def _(block):
        @pl.when(block < blocks - 1)
        def _():
            each(fetches, block + 1, lambda copy: copy.start())
            arrive(block + 1)

        @pl.loop(0, per)
        def _(j):
            for copy in share(block * per + j):
                copy.wait_recv()

        each(fetches, block, lambda copy: copy.wait())

        @pl.when(block >= 2)
        def _():
            each(results, block - 2, lambda copy: copy.wait())

        work(block)
        each(results, block, lambda copy: copy.start())
        for copy in hand(block):
            copy.start()

        @pl.when(block >= 1)
        def _():
            finish(block - 1)

    finish(blocks - 1)
    for block in (blocks - 2, blocks - 1):
        each(results, block, lambda copy: copy.wait())

    @pl.loop(0, blocks)
    def _(block):
        for copy in hand(block):
            copy.wait_send()

    @pl.loop(0, 64)
    def _(k):
        for copy in share(k):
            copy.wait_send()

        @pl.when(k > 0)
        def _():
            for copy in packet(k):
                copy.wait_send()
            for copy in reply(k):
                copy.wait_recv()
                copy.wait_send()

    for copy in keep_back():
        copy.wait()


def run_experts(main, tail, grads_main, grads_extra, gate_w, up_w, down_w):
    wide = gate_w.shape[0]
    grad = jax.ShapeDtypeStruct((wide, D), F32)

    def pair(count):
        return [pltpu.VMEM((count, 2, 8, D), BF16), pltpu.VMEM((count, 2, 8, TAIL), BF16)]

    staged = [pltpu.VMEM((2, 16, 2, 8, D), BF16), pltpu.VMEM((2, 16, 2, 8, 256), BF16)]
    return pl.pallas_call(
        moe_kernel,
        out_shape=(
            jax.ShapeDtypeStruct((2, 32, 2, 8, D), BF16),
            jax.ShapeDtypeStruct((2, 32, 2, 8, TAIL), BF16),
            jax.ShapeDtypeStruct((4, 32, 2, 8, D), BF16),
            jax.ShapeDtypeStruct((4, 32, 2, 8, 256), BF16),
            grad,
            grad,
            grad,
        ),
        in_specs=[ANY] * 4 + [VMEM] * 3,
        out_specs=(ANY,) * 4 + (VMEM,) * 3,
        scratch_shapes=pair(64)
        + pair(64)
        + staged
        + staged
        + pair(64)
        + pair(64)
        + pair(64)
        + [DMA((2,))]
        + [DMA((2, 64))] * 4
        + [DMA((2, 2, 16))] * 2
        + [DMA((2, 8))] * 2
        + [DMA((2,))]
        + [DMA((2, 64))] * 2,
        compiler_params=params(2, 60),
        cost_estimate=cost(90 << 20, 33 << 30),
    )(main, tail, grads_main, grads_extra, gate_w, up_w, down_w)


def rms_forward(values, gain):
    factor = lax.rsqrt(jnp.mean(values * values, -1, keepdims=True) + EPSILON)
    normed = values * factor
    return (normed, factor, normed * gain)


def rms_values(grad_output, normed, factor, gain):
    grad_normed = grad_output * gain
    return factor * (grad_normed - normed * jnp.mean(grad_normed * normed, -1, keepdims=True))


def split(values):
    high = values.astype(BF16)
    return high, (values - high.astype(F32)).astype(BF16)


def body(
    layer_in,
    w_query,
    w_key,
    w_value,
    w_out,
    norm_attn,
    norm_moe,
    rel_table,
    w_router,
    expert_gate,
    expert_up,
    expert_down,
    routes,
    rel_bucket,
    cotangent,
):
    tokens = 2 * ROWS
    seq = lax.axis_index("seq")

    route_flat = routes.reshape(tokens, 2)
    expert_ids = jnp.arange(EXPERTS, dtype=jnp.int32)
    choose_hot = route_flat[:, :, None] == expert_ids[None, None, :]
    order_hot = choose_hot.transpose(1, 0, 2).reshape(2 * tokens, EXPERTS).astype(jnp.int32)
    earlier = jnp.cumsum(order_hot, 0) - order_hot
    slot_order = jnp.sum(earlier * order_hot, -1)
    dropped = jnp.sum(order_hot * (slot_order >= CAP)[:, None].astype(jnp.int32), 0)
    tallies = jnp.stack([jnp.sum(order_hot, 0), dropped])
    slots = slot_order.reshape(2, tokens).transpose(1, 0)
    columns = jnp.arange(EXPERTS * MAIN, dtype=jnp.int32)
    main_place = jnp.where(slots < MAIN, route_flat * MAIN + slots, -1)
    hot_main = main_place[:, :, None] == columns[None, None, :]
    extra_place = jnp.where(
        (slots >= MAIN) & (slots < CAP), route_flat * 4 + slots - MAIN, -1
    )
    hot_extra = extra_place[:, :, None] == (columns // 4)[None, None, :]
    quarter = jnp.arange(4, dtype=jnp.int32)
    quarter_hot = quarter[:, None] == (columns % 4)[None, :]

    def spread(values_k):
        hot_m = hot_main.astype(BF16)
        hot_x = (hot_extra[None] & quarter_hot[:, None, None, :]).astype(BF16)
        main = jnp.einsum("tkc,td->cd", hot_m, values_k, preferred_element_type=F32)
        extra = jnp.einsum(
            "mtkc,tmd->cd", hot_x, values_k.reshape(tokens, 4, 256), preferred_element_type=F32
        )
        return main.astype(BF16), extra.astype(BF16)

    slab = jnp.concatenate(
        [
            w_query,
            w_key,
            w_value,
            w_out,
            w_router,
            norm_attn[:, None],
            norm_moe[:, None],
            jnp.pad(rel_table[None], ((0, 7), (0, 0))),
            jnp.pad(tallies.astype(BF16), ((0, 6), (0, 0))),
            jnp.zeros((8, 186), BF16),
        ],
        1,
    )
    grad_main, grad_extra = spread(cotangent.reshape(tokens, D))
    full, items, grads_main, grads_extra = gather_all(
        slab,
        layer_in.reshape(2, 16, 8, D),
        grad_main.reshape(EXPERTS, 2, 8, D),
        grad_extra.reshape(EXPERTS, 2, 8, 256),
    )

    full = full.reshape(D, SLAB)
    full_query, full_kv, full_out = full[:, :D], full[:, D : 3 * D], full[:, 3 * D : 4 * D]
    smalls = full[:, 4 * D :]
    full_router = smalls[:, 0:32]
    gain_attn = smalls[:, 32].astype(F32)
    gain_moe = smalls[:, 33].astype(F32)
    smalls = smalls.reshape(128, 8, 256)
    table = smalls[:, 0, 34:38].reshape(BUCKETS, HEADS)
    totals = jnp.sum(smalls[:, 0:2, 38:70].astype(F32), 0).astype(jnp.int32)

    inputs = layer_in.astype(F32).reshape(tokens, D)
    own_hidden = rms_forward(inputs, gain_attn)[2].astype(BF16)
    all_inputs = items.astype(F32).reshape(4 * tokens, D)
    normed_one, factor_one, hidden_one = rms_forward(all_inputs, gain_attn)
    hidden_one = hidden_one.astype(BF16)
    query = dot(own_hidden, full_query).astype(BF16)
    kv_all = dot(hidden_one, full_kv).astype(BF16)
    bucket_hot = (rel_bucket[:, None] == jnp.arange(BUCKETS, dtype=jnp.int32)[None, :]).astype(BF16)
    offsets = jnp.einsum("ob,bh->ho", bucket_hot, table, preferred_element_type=F32)
    offsets = jnp.pad(offsets, ((0, 0), (0, 1)))
    windows = lax.dynamic_slice(offsets, (0, LENGTH - ROWS - seq * ROWS), (HEADS, 640))
    mixed = attend(
        windows.reshape(HEADS // 2, 2, 640),
        query.reshape(2, ROWS // 8, 8, D),
        kv_all.reshape(2, LENGTH // 8, 8, 2 * D),
    ).reshape(tokens, D)
    resid = inputs + dot(mixed, full_out)
    normed_two, factor_two, hidden_two = rms_forward(resid, gain_moe)
    hidden_two = hidden_two.astype(BF16)
    logits = dot(hidden_two, full_router)
    chosen = jnp.sum(jnp.where(choose_hot, logits[:, None, :], 0.0), -1)
    gates = jax.nn.softmax(chosen, -1)

    rows_main, rows_extra = spread(hidden_two)
    gate_main = jnp.sum(jnp.where(hot_main, gates[:, :, None], 0.0), (0, 1))
    gate_extra = jnp.sum(jnp.where(hot_extra, gates[:, :, None], 0.0), (0, 1))
    lanes = jnp.stack(split(gate_main) + split(gate_extra), -1)
    rows_tail = jnp.concatenate([rows_extra, jnp.pad(lanes, ((0, 0), (0, 124)))], -1)
    grads_main = lax.all_gather(grads_main, "seq", axis=0, tiled=False)
    grads_extra = lax.all_gather(grads_extra, "seq", axis=0, tiled=False)
    returned, returned_tail, out_main, out_extra, *expert_grads = run_experts(
        rows_main.reshape(EXPERTS, 2, 8, D),
        rows_tail.reshape(EXPERTS, 2, 8, TAIL),
        grads_main,
        grads_extra,
        expert_gate[0].T,
        expert_up[0].T,
        expert_down[0],
    )
    grad_gate, grad_up, grad_down = expert_grads[0].T, expert_grads[1].T, expert_grads[2]

    hot_both = jnp.sum(hot_main.astype(BF16), 1)
    hot_extra_both = jnp.sum(hot_extra.astype(BF16), 1)
    quarters = [hot_extra_both * quarter_hot[m][None, :].astype(BF16) for m in range(4)]
    back = returned.reshape(2 * EXPERTS * MAIN, D)
    back_tail = returned_tail.reshape(2 * EXPERTS * MAIN, TAIL)
    from_main = dot(jnp.concatenate([hot_both, hot_both], 1), back)
    from_extra = jnp.concatenate(
        [dot(jnp.concatenate([hot, hot], 1), back_tail[:, :256]) for hot in quarters], 1
    )
    grad_from_experts = from_main + from_extra
    returned_gates = back_tail[:, 256:258].astype(F32).reshape(2, EXPERTS * MAIN, 2)
    returned_gates = returned_gates[0] + returned_gates[1]
    grad_gates = jnp.sum(jnp.where(hot_main, returned_gates[:, 0], 0.0), -1) + 0.25 * jnp.sum(
        jnp.where(hot_extra, returned_gates[:, 1], 0.0), -1
    )

    grad_final = cotangent.astype(F32).reshape(tokens, D)
    grad_chosen = gates * (grad_gates - jnp.sum(gates * grad_gates, -1, keepdims=True))
    grad_logits = jnp.sum(jnp.where(choose_hot, grad_chosen[:, :, None], 0.0), 1).astype(BF16)
    grad_router_part = dot(hidden_two, grad_logits, TN)
    grad_hidden_two = grad_from_experts + dot(grad_logits, full_router, NT)
    grad_gain_moe = jnp.sum(grad_hidden_two * normed_two, 0)
    grad_resid = grad_final + rms_values(grad_hidden_two, normed_two, factor_two, gain_moe)
    grad_attended = gather_items(grad_resid.astype(BF16).reshape(2, 16, 8, D))
    grad_attended, out_main, out_extra = lax.optimization_barrier(
        (grad_attended, out_main, out_extra)
    )
    out_main = lax.psum_scatter(out_main, "seq", scatter_dimension=0, tiled=False)
    out_extra = lax.psum_scatter(out_extra, "seq", scatter_dimension=0, tiled=False)
    grad_attended = grad_attended.reshape(4 * tokens, D)

    first = seq * 256
    own_query, own_key, own_value = [
        lax.dynamic_slice(full, (0, index * D + first), (D, 256)) for index in range(3)
    ]
    own_out = lax.dynamic_slice(full, (first, 3 * D), (256, D))
    head_query = dot(hidden_one, own_query).astype(BF16)
    head_key = lax.dynamic_slice(kv_all, (0, first), (4 * tokens, 256))
    head_value = lax.dynamic_slice(kv_all, (0, D + first), (4 * tokens, 256))
    grad_mixed = dot(grad_attended, own_out, NT).astype(BF16)
    head_offsets = lax.dynamic_slice(offsets, (seq * 4, 0), (4, 1024))
    head_windows = jnp.stack(
        [
            head_offsets[:, LENGTH - ROWS - block * ROWS : LENGTH - ROWS - block * ROWS + 640]
            for block in range(4)
        ],
        1,
    ).reshape(2, 2, 4, 640)
    shape = (2, LENGTH // 8, 8, 256)
    head_mixed, dquery, dkey, dvalue, dbias = attend_back(
        head_windows,
        head_query.reshape(shape),
        head_key.reshape(shape),
        head_value.reshape(shape),
        grad_mixed.reshape(shape),
    )
    grad_offsets = jnp.sum(dbias, 0).reshape(4, 1024)[:, :1023]
    grad_table = jnp.einsum(
        "ob,ho->bh", bucket_hot.astype(F32), grad_offsets, precision=lax.Precision.HIGHEST
    )
    heads_grad = jnp.concatenate([dquery, dkey, dvalue], -1).reshape(4 * tokens, 768)
    own_weights = jnp.concatenate([own_query, own_key, own_value], 1)
    grad_qkv = dot(hidden_one, heads_grad, TN).astype(BF16).reshape(32, 32, 768)
    grad_out = dot(head_mixed.reshape(4 * tokens, 256), grad_attended, TN).astype(BF16)
    grad_out = grad_out.reshape(32, 8, 4, 256).transpose(0, 2, 1, 3).reshape(32, 32, 256)
    part_hidden = dot(heads_grad, own_weights, NT)
    grad_gain_attn = jnp.sum(part_hidden * normed_one, 0)
    table_lanes = (
        (jnp.arange(32, dtype=jnp.int32) == seq * 8)[None, :, None] * grad_table[:, None, :]
    )
    smalls_grad = jnp.concatenate(
        [
            grad_router_part.reshape(32, 32, 32),
            grad_gain_attn.reshape(32, 32, 1),
            grad_gain_moe.reshape(32, 32, 1),
            table_lanes,
            jnp.zeros((32, 32, 90), F32),
        ],
        -1,
    ).astype(BF16)
    rest = jnp.concatenate([smalls_grad, grad_out], -1)
    mine, other, small_sums, wide_sums, out_main, out_extra = reduce_grads(
        grad_qkv.reshape(4, 2, 4, 4, 8, 768),
        rest.reshape(4, 2, 4, 4, 8, 384),
        part_hidden.astype(BF16).reshape(2, 4, 16, 8, D),
        out_main,
        out_extra,
    )

    gated_main = split(jnp.sum(jnp.where(hot_main, gates[:, :, None], 0.0), 1))
    gated_extra = split(jnp.sum(jnp.where(hot_extra, gates[:, :, None], 0.0), 1))
    out_main = out_main.reshape(EXPERTS * MAIN, D)
    out_extra = out_extra.reshape(EXPERTS * MAIN, 256)
    moe_out = dot(
        jnp.concatenate(gated_main, 1), jnp.concatenate([out_main, out_main], 0)
    ) + jnp.concatenate(
        [
            dot(
                jnp.concatenate([part * quarter_hot[m][None, :].astype(BF16) for part in gated_extra], 1),
                jnp.concatenate([out_extra, out_extra], 0),
            )
            for m in range(4)
        ],
        1,
    )
    layer_out = (resid + moe_out).astype(BF16).reshape(2, ROWS, D)


    wide_sums = wide_sums.transpose(1, 0, 2).reshape(8, D)
    moves = [
        (dp * 4 + own, (8 * own + dp // 4) * 4 + dp % 4) for dp in range(32) for own in range(4)
    ]
    grad_out_own = lax.ppermute(wide_sums, ("dp", "seq"), moves)
    grad_weights = [
        small_sums[:, :, index * 256 : index * 256 + 256].transpose(1, 0, 2).reshape(8, D)
        for index in range(3)
    ]
    small_own = jnp.sum(small_sums[:, :, 768:], 0)
    grad_hidden_one = (mine + other.astype(F32)).reshape(tokens, D)
    own_normed, own_factor, _ = rms_forward(inputs, gain_attn)
    grad_in = grad_resid + rms_values(grad_hidden_one, own_normed, own_factor, gain_attn)
    return (
        layer_out,
        grad_in.reshape(2, ROWS, D),
        grad_weights[0],
        grad_weights[1],
        grad_weights[2],
        grad_out_own,
        small_own[:, 32],
        small_own[:, 33],
        small_own[0, 34:38],
        small_own[:, 0:32],
        grad_gate[None],
        grad_up[None],
        grad_down[None],
        totals,
    )


def solution(mesh):
    rows = P(("dp", "seq"), None)
    vector = P(("dp", "seq"))
    block = P("dp", "seq", None)
    wide = P("dp", None, "seq")
    return jax.shard_map(
        body,
        mesh=mesh,
        in_specs=(
            block,
            rows,
            rows,
            rows,
            rows,
            vector,
            vector,
            vector,
            rows,
            wide,
            wide,
            block,
            block,
            P(),
            block,
        ),
        out_specs=(
            block,
            block,
            rows,
            rows,
            rows,
            rows,
            vector,
            vector,
            vector,
            rows,
            wide,
            wide,
            block,
            P(),
        ),
        check_vma=False,
    )
```

```python
import math

import jax
import jax.numpy as jnp
from jax import lax
from jax.experimental import pallas as pl
from jax.experimental.pallas import tpu as pltpu
from jax.sharding import PartitionSpec as P

MESH = pl.DeviceIdType.MESH
ANY = pl.BlockSpec(memory_space=pl.ANY)
VMEM = pl.BlockSpec(memory_space=pltpu.VMEM)
DMA = pltpu.SemaphoreType.DMA
F32 = jnp.float32
BF16 = jnp.bfloat16

D = 1024
HEADS = 16
SIZE = 64
BUCKETS = 32
EXPERTS = 32
LENGTH = 512
ROWS = 128
CAP = 20
MAIN = 16
EPSILON = 1e-06

SLAB = 4 * 1024 + 256
PARTS = ((0, 1536), (1536, 1408), (2944, 1408))
ORDERS = ("xyz", "yzx", "zxy")
TAIL = 256 + 128
PACK = 1024 + 256
GRAD = 3 * 256 + 128 + 256
THIRD = GRAD // 3


def div(a, b):
    return lax.div(a, jnp.int32(b))


def rem(a, b):
    return lax.rem(a, jnp.int32(b))


def place():
    dp, seq = lax.axis_index("dp"), lax.axis_index("seq")
    x = div(seq, 2) * 2 + rem(div(dp, 4), 2)
    return x, div(dp, 8), rem(dp, 4), rem(seq, 2)


def device(x, y, z, core):
    return ((y * 2 + rem(x, 2)) * 4 + z, div(x, 2) * 2 + core)


def greet(devices):
    barrier = pltpu.get_barrier_semaphore()
    for one in devices:
        pl.semaphore_signal(barrier, inc=1, device_id=one, device_id_type=MESH)
    pl.semaphore_wait(barrier, len(devices))


def remote(src, dst, send, recv, to):
    return pltpu.make_async_remote_copy(
        src_ref=src, dst_ref=dst, send_sem=send, recv_sem=recv, device_id=to, device_id_type=MESH
    )


def params(collective, megabytes):
    return pltpu.CompilerParams(
        collective_id=collective, has_side_effects=True, vmem_limit_bytes=megabytes << 20
    )


def cost(sent, flops=0):
    return pl.CostEstimate(flops=flops, bytes_accessed=sent, transcendentals=0)


def seq_gather_start(own, full, relay, sems):
    local, send, recv = sems
    x, y, z, core = place()
    right, left = device(rem(x + 1, 4), y, z, core), device(rem(x + 3, 4), y, z, core)
    sibling = device(x, y, z, 1 - core)
    me = div(x, 2) * 2 + core
    mine = pltpu.make_async_copy(own, full.at[:, me], local)
    copies = [
        remote(own, full.at[:, me], send.at[0], recv.at[0], sibling),
        remote(own.at[0], relay.at[0], send.at[1], recv.at[1], right),
        remote(own.at[1], relay.at[1], send.at[2], recv.at[2], left),
    ]
    mine.start()
    for copy in copies[1:] + copies[:1]:
        copy.start()
    return mine, copies


def seq_gather_finish(state, full, relay, sems):
    local, send, recv = sems
    mine, copies = state
    x, y, z, core = place()
    right, left = device(rem(x + 1, 4), y, z, core), device(rem(x + 3, 4), y, z, core)
    sibling = device(x, y, z, 1 - core)
    from_left = div(rem(x + 3, 4), 2) * 2 + core
    from_right = div(rem(x + 1, 4), 2) * 2 + core
    partner = rem(div(x, 2) + 1, 2) * 2 + core
    onward = [
        remote(relay.at[0], full.at[0, from_left], send.at[3], recv.at[3], right),
        remote(relay.at[1], full.at[1, from_right], send.at[4], recv.at[4], left),
    ]
    across = [
        remote(full.at[0, partner], full.at[0, partner], send.at[5], recv.at[5], sibling),
        remote(full.at[1, partner], full.at[1, partner], send.at[6], recv.at[6], sibling),
    ]
    for item in range(2):
        copies[1 + item].wait_recv()
        onward[item].start()
    for item in range(2):
        onward[item].wait_recv()
        across[item].start()
    mine.wait()
    copies[0].wait_recv()
    for copy in across:
        copy.wait_recv()
    for copy in copies + onward + across:
        copy.wait_send()


def chips(k):
    x, y, z, core = place()
    kx, ky, kz = div(k, 16), rem(div(k, 4), 4), rem(k, 4)
    ahead = (rem(x + kx, 4), rem(y + ky, 4), rem(z + kz, 4))
    behind = (rem(x + 4 - kx, 4), rem(y + 4 - ky, 4), rem(z + 4 - kz, 4))
    return ahead, behind


def greet_chips():
    x, y, z, core = place()
    barrier = pltpu.get_barrier_semaphore()

    @pl.loop(1, 64)
    def _(k):
        ahead, _ = chips(k)
        pl.semaphore_signal(barrier, inc=1, device_id=device(*ahead, core), device_id_type=MESH)

    pl.semaphore_signal(barrier, inc=1, device_id=device(x, y, z, 1 - core), device_id_type=MESH)
    pl.semaphore_wait(barrier, 64)


def peers(k):
    x, y, z, core = place()
    kx, ky, kz = div(k, 16), rem(div(k, 4), 4), rem(k, 4)
    return device(div(x, 2) * 2 + rem(rem(x, 2) + kx, 2), rem(y + ky, 4), rem(z + kz, 4), core)


def greet_peers(others):
    barrier = pltpu.get_barrier_semaphore()

    @pl.loop(1, 32)
    def _(k):
        pl.semaphore_signal(barrier, inc=1, device_id=peers(k), device_id_type=MESH)

    for one in others:
        pl.semaphore_signal(barrier, inc=1, device_id=one, device_id_type=MESH)
    pl.semaphore_wait(barrier, 31 + len(others))


class Exchange:
    def __init__(self, slabs, rows, local, send, recv):
        self.slabs, self.rows = slabs, rows
        self.local, self.send, self.recv = local, send, recv
        self.dp = lax.axis_index("dp")

    def packet(self, k):
        to = peers(k)
        return [
            remote(slab.at[to[0]], rows.at[self.dp], self.send.at[i, k], self.recv.at[i, k], to)
            for i, (slab, rows) in enumerate(zip(self.slabs, self.rows))
        ]

    def kept(self):
        return [
            pltpu.make_async_copy(slab.at[self.dp], rows.at[self.dp], self.local.at[i])
            for i, (slab, rows) in enumerate(zip(self.slabs, self.rows))
        ]

    def start(self, first, last):
        @pl.loop(first, last)
        def _(k):
            for copy in self.packet(k):
                copy.start()

    def keep(self):
        for copy in self.kept():
            copy.start()

    def finish(self):
        @pl.loop(1, 32)
        def _(k):
            for copy in self.packet(k):
                copy.wait_recv()
                copy.wait_send()

        for copy in self.kept():
            copy.wait()


EXCHANGE_SEMS = [DMA((2,)), DMA((2, 32)), DMA((2, 32))]


def gather_kernel(
    slab,
    own,
    slabs,
    full,
    items,
    arrived_slabs,
    relay,
    local,
    send,
    recv,
    near_send,
    near_recv,
    seq_local,
    seq_send,
    seq_recv,
    *exchange_sems,
):
    x, y, z, core = place()
    at = {"x": x, "y": y, "z": z}
    sibling = device(x, y, z, 1 - core)

    def moved(axis, by):
        return dict(at, **{axis: rem(at[axis] + by, 4)})

    def who(spot):
        return device(spot["x"], spot["y"], spot["z"], core)

    greet_peers([who(moved(axis, by)) for axis in "xyz" for by in (1, 3)] + [sibling])
    packets = Exchange((slabs,), (arrived_slabs,), *exchange_sems)

    def block(spot, whole, first, width):
        every = slice(None)
        row = every if "y" in whole else spot["y"]
        depth = every if "z" in whole else spot["z"]
        near, far = every, every
        if "x" not in whole:
            near, far = rem(spot["x"], 2), div(spot["x"], 2)
        return full.at[row, near, depth, far, core, :, pl.ds(first, width)]

    near = []

    def share(ref):
        k = len(near)
        copy = remote(ref, ref, near_send.at[k], near_recv.at[k], sibling)
        copy.start()
        near.append(copy)

    own_place = full.at[y, rem(x, 2), z, div(x, 2), core]
    mine = pltpu.make_async_copy(slab, own_place, local)
    mine.start()
    sems = (seq_local, seq_send, seq_recv)
    state = seq_gather_start(own, items, relay, sems)
    packets.keep()
    mine.wait()
    share(own_place)
    sent = []
    for stage in range(3):
        steps = []
        for part in range(3):
            axis, whole = ORDERS[part][stage], ORDERS[part][:stage]
            first, width = PARTS[part]
            near_half = 768
            k = (part * 3 + stage) * 4
            right, left = who(moved(axis, 1)), who(moved(axis, 3))
            here = block(at, whole, first, width)
            there_left, there_right = moved(axis, 3), moved(axis, 1)
            part_left = block(there_left, whole, first, near_half)
            part_right = block(there_right, whole, first + near_half, width - near_half)
            copies = [
                remote(here, here, send.at[k], recv.at[k], right),
                remote(here, here, send.at[k + 1], recv.at[k + 1], left),
                remote(part_left, part_left, send.at[k + 2], recv.at[k + 2], right),
                remote(part_right, part_right, send.at[k + 3], recv.at[k + 3], left),
            ]
            copies[0].start()
            copies[1].start()
            opposite = moved(axis, 2)
            steps.append(
                (
                    copies,
                    [
                        block(there_left, whole, first, width),
                        block(there_right, whole, first, width),
                        block(opposite, whole, first, near_half),
                        block(opposite, whole, first + near_half, width - near_half),
                    ],
                )
            )
            sent.extend(copies)
        packets.start(*((1, 11), (11, 22), (22, 32))[stage])
        for copies, arrived in steps:
            for k in range(2):
                copies[k].wait_recv()
                copies[k + 2].start()
                share(arrived[k])
        for copies, arrived in steps:
            for k in range(2, 4):
                copies[k].wait_recv()
                share(arrived[k])
    seq_gather_finish(state, items, relay, sems)
    packets.finish()
    for copy in near:
        copy.wait_recv()
    for copy in sent + near:
        copy.wait_send()


def gather_all(slab, own, slabs):
    return pl.pallas_call(
        gather_kernel,
        out_shape=(
            jax.ShapeDtypeStruct((4, 2, 4, 2, 2, 8, SLAB), BF16),
            jax.ShapeDtypeStruct((2, 4, 16, 8, D), BF16),
            jax.ShapeDtypeStruct((32, 2, 8, PACK), BF16),
        ),
        in_specs=[ANY] * 3,
        out_specs=(ANY,) * 3,
        scratch_shapes=[
            pltpu.VMEM((2, 16, 8, D), BF16),
            DMA(()),
            DMA((36,)),
            DMA((36,)),
            DMA((37,)),
            DMA((37,)),
            DMA(()),
            DMA((7,)),
            DMA((7,)),
            *EXCHANGE_SEMS,
        ],
        compiler_params=params(0, 32),
        cost_estimate=cost(90 << 20),
    )(slab, own, slabs)


def items_kernel(own, full, relay, local, send, recv):
    x, y, z, core = place()
    greet(
        [
            device(rem(x + 1, 4), y, z, core),
            device(rem(x + 3, 4), y, z, core),
            device(x, y, z, 1 - core),
        ]
    )
    sems = (local, send, recv)
    state = seq_gather_start(own, full, relay, sems)
    seq_gather_finish(state, full, relay, sems)


def gather_items(own):
    return pl.pallas_call(
        items_kernel,
        out_shape=jax.ShapeDtypeStruct((2, 4, 16, 8, D), BF16),
        in_specs=[ANY],
        out_specs=ANY,
        scratch_shapes=[pltpu.VMEM((2, 16, 8, D), BF16), DMA(()), DMA((7,)), DMA((7,))],
        compiler_params=params(1, 32),
        cost_estimate=cost(20 << 20),
    )(own)


def grads_kernel(
    heads,
    rest,
    part,
    outs,
    mine,
    other,
    small,
    wide,
    arrived_outs,
    own,
    got,
    relay,
    first_in,
    first_sum,
    second_in,
    total,
    own_local,
    near_send,
    near_recv,
    relay_send,
    relay_recv,
    first_local,
    first_send,
    first_recv,
    second_send,
    second_recv,
    last_local,
    last_send,
    last_recv,
    *exchange_sems,
):
    x, y, z, core = place()
    my_dp, my_seq = device(x, y, z, core)
    sibling = device(x, y, z, 1 - core)
    right, left = device(rem(x + 1, 4), y, z, core), device(rem(x + 3, 4), y, z, core)
    here = div(x, 2)
    away = 1 - here

    greet_peers([(my_dp, rem(my_seq + step, 4)) for step in range(1, 4)] + [right, left])

    shares = []
    for k, side in enumerate((away, here)):
        shares.append(
            (
                remote(
                    part.at[:, side * 2 + 1 - core],
                    got.at[k],
                    near_send.at[k],
                    near_recv.at[k],
                    sibling,
                ),
                pltpu.make_async_copy(part.at[:, side * 2 + core], own.at[k], own_local.at[k]),
            )
        )
        for copy in shares[k]:
            copy.start()

    near, every = rem(x, 2), slice(None)
    sizes = (4, 4, 2)
    low, high = pl.ds(0, THIRD), pl.ds(THIRD, THIRD)

    def piece(index, step):
        if index == 0:
            return heads.at[rem(y + step, 4), :, :, :, :, low]
        if index == 1:
            return heads.at[:, :, rem(z + step, 4), :, :, high]
        return rest.at[:, rem(near + step, 2)]

    def along(index, step):
        if index == 0:
            return device(x, rem(y + step, 4), z, core)
        if index == 1:
            return device(x, y, rem(z + step, 4), core)
        return device(here * 2 + rem(near + step, 2), y, z, core)

    firsts, keeps = [], []
    for index in range(3):
        for step in range(sizes[index]):
            k = index * 4 + step
            if step == 0:
                copy = pltpu.make_async_copy(
                    piece(index, 0), first_in[index].at[0], first_local.at[index]
                )
                keeps.append(copy)
            else:
                copy = remote(
                    piece(index, step),
                    first_in[index].at[step],
                    first_send.at[k],
                    first_recv.at[k],
                    along(index, step),
                )
                firsts.append((index, copy))
            copy.start()
    packets = Exchange((outs,), (arrived_outs,), *exchange_sems)
    packets.start(1, 32)
    packets.keep()

    shares[0][1].wait()
    shares[0][0].wait_recv()
    hops = [
        remote(own.at[0, 0], relay.at[0], relay_send.at[0], relay_recv.at[0], right),
        remote(own.at[0, 1], relay.at[1], relay_send.at[1], relay_recv.at[1], left),
        remote(relay.at[0], other.at[0], relay_send.at[2], relay_recv.at[2], right),
        remote(relay.at[1], other.at[1], relay_send.at[3], relay_recv.at[3], left),
    ]
    for item in range(2):

        @pl.loop(0, 8)
        def _(row):
            rows = pl.ds(row * 2, 2)
            summed = own[0, item, rows].astype(F32) + got[0, item, rows].astype(F32)
            own[0, item, rows] = summed.astype(BF16)

        hops[item].start()
    shares[1][1].wait()
    shares[1][0].wait_recv()
    for item in range(2):

        @pl.loop(0, 8)
        def _(row):
            rows = pl.ds(row * 2, 2)
            mine[item, rows] = own[1, item, rows].astype(F32) + got[1, item, rows].astype(F32)

    for item in range(2):
        hops[item].wait_recv()
        hops[2 + item].start()

    def to_second(index, k):
        if index == 0:
            a, b = rem(near + div(k, 4), 2), rem(z + rem(k, 4), 4)
            return (a, b), device(here * 2 + a, y, b, core)
        if index == 1:
            a, b = rem(y + rem(k, 4), 4), rem(near + div(k, 4), 2)
            return (a, b), device(here * 2 + b, a, z, core)
        a, b = rem(y + div(k, 4), 4), rem(z + rem(k, 4), 4)
        return (a, b), device(x, a, b, core)

    def second(index, k):
        spot, to = to_second(index, k)
        slot = index * 8 + k
        return remote(
            first_sum[index].at[spot],
            second_in.at[slot],
            second_send.at[slot],
            second_recv.at[slot],
            to,
        )

    counts = (8, 8, 16)
    for index in range(3):
        keeps[index].wait()
        for which, copy in firsts:
            if which == index:
                copy.wait_recv()
        held, summed = first_in[index], first_sum[index]
        rows, columns = summed.shape[0], summed.shape[1]

        @pl.loop(0, rows)
        def _(a):
            for b in range(columns):
                value = held[0, a, b].astype(F32)
                for step in range(1, sizes[index]):
                    value = value + held[step, a, b].astype(F32)
                summed[a, b] = value.astype(BF16)

        @pl.loop(1, counts[index])
        def _(k):
            second(index, k).start()

    for index in range(3):
        columns = pl.ds(index * THIRD, THIRD)
        total[:, :, columns] = first_sum[index][to_second(index, jnp.int32(0))[0]].astype(F32)

        @pl.loop(1, counts[index])
        def _(k):
            second(index, k).wait_recv()
            total[:, :, columns] += second_in[index * 8 + k].astype(F32)

    columns = 3 * 256 + 128
    last = []
    for step in range(1, 4):
        seq = rem(my_seq + step, 4)
        copy = remote(
            total.at[seq, :, pl.ds(0, columns)],
            small.at[my_seq],
            last_send.at[step],
            last_recv.at[step],
            (my_dp, seq),
        )
        copy.start()
        last.append(copy)
    keep = pltpu.make_async_copy(
        total.at[my_seq, :, pl.ds(0, columns)],
        small.at[my_seq],
        last_local,
    )
    keep.start()
    wide[...] = total[:, :, columns:]
    keep.wait()
    for copy in last:
        copy.wait_recv()
    for item in range(2):
        hops[2 + item].wait_recv()
    packets.finish()
    for copy in last + hops + [share[0] for share in shares]:
        copy.wait_send()

    for _, copy in firsts:
        copy.wait_send()
    for index in range(3):

        @pl.loop(1, counts[index])
        def _(k):
            second(index, k).wait_send()


def reduce_grads(heads, rest, part, outs):
    columns = 3 * 256 + 128
    return pl.pallas_call(
        grads_kernel,
        out_shape=(
            jax.ShapeDtypeStruct((2, 16, 8, D), F32),
            jax.ShapeDtypeStruct((2, 16, 8, D), BF16),
            jax.ShapeDtypeStruct((4, 8, columns), F32),
            jax.ShapeDtypeStruct((4, 8, 256), F32),
            jax.ShapeDtypeStruct((32, 2, 8, PACK), BF16),
        ),
        in_specs=[ANY] * 4,
        out_specs=(VMEM, ANY, VMEM, VMEM, ANY),
        scratch_shapes=[
            pltpu.VMEM((2, 2, 16, 8, D), BF16),
            pltpu.VMEM((2, 2, 16, 8, D), BF16),
            pltpu.VMEM((2, 16, 8, D), BF16),
            [
                pltpu.VMEM((4, 2, 4, 4, 8, THIRD), BF16),
                pltpu.VMEM((4, 4, 2, 4, 8, THIRD), BF16),
                pltpu.VMEM((2, 4, 4, 4, 8, THIRD), BF16),
            ],
            [
                pltpu.VMEM((2, 4, 4, 8, THIRD), BF16),
                pltpu.VMEM((4, 2, 4, 8, THIRD), BF16),
                pltpu.VMEM((4, 4, 4, 8, THIRD), BF16),
            ],
            pltpu.VMEM((32, 4, 8, THIRD), BF16),
            pltpu.VMEM((4, 8, GRAD), F32),
            DMA((2,)),
            DMA((2,)),
            DMA((2,)),
            DMA((4,)),
            DMA((4,)),
            DMA((3,)),
            DMA((12,)),
            DMA((12,)),
            DMA((32,)),
            DMA((32,)),
            DMA(()),
            DMA((4,)),
            DMA((4,)),
            *EXCHANGE_SEMS,
        ],
        compiler_params=params(4, 48),
        cost_estimate=cost(60 << 20),
    )(heads, rest, part, outs)


NT = (((1,), (1,)), ((), ()))
TN = (((0,), (0,)), ((), ()))


def dot(a, b, dims=None):
    if dims is None:
        return jnp.dot(a, b, preferred_element_type=F32)
    return lax.dot_general(a, b, dims, preferred_element_type=F32)


def bias_rows(window):
    return pltpu.roll(
        jnp.broadcast_to(window, (ROWS, 640)), 640 - 127, 1, stride=1, stride_axis=0
    )[:, :LENGTH]


def flat(rows):
    return rows.astype(F32).reshape(rows.shape[0] * 8, 128).astype(BF16)


def tiled(rows):
    return rows.reshape(rows.shape[0] // 8, 8, 128).astype(BF16)


def softmax(scores):
    powers = jnp.exp(scores - jnp.max(scores, -1, keepdims=True))
    return powers * (1.0 / jnp.sum(powers, -1, keepdims=True))


def forward_kernel(window, query, key, value, mixed):
    low = lax.broadcasted_iota(jnp.int32, (ROWS, 128), 1) < SIZE
    biases = [bias_rows(window[0, head : head + 1]) for head in range(2)]
    for item in range(2):
        queries = query[item].astype(F32).reshape(ROWS, 128) * SIZE**-0.5
        keys, values = flat(key[item]), flat(value[item])
        results = []
        for head in range(2):
            own = low if head == 0 else ~low
            one = jnp.where(own, queries, 0.0).astype(BF16)
            scores = dot(one, keys, NT) + biases[head]
            results.append(dot(softmax(scores).astype(BF16), values))
        mixed[item] = tiled(jnp.where(low, results[0], results[1]))


def attend(windows, query, key_value):
    def block(rows, first=0):
        return pl.BlockSpec((2, rows // 8, 8, 128), lambda pair: (0, 0, 0, first + pair))

    return pl.pallas_call(
        forward_kernel,
        grid=(HEADS // 2,),
        out_shape=jax.ShapeDtypeStruct((2, ROWS // 8, 8, D), BF16),
        in_specs=[
            pl.BlockSpec((1, 2, 640), lambda pair: (pair, 0, 0)),
            block(ROWS),
            block(LENGTH),
            block(LENGTH, HEADS // 2),
        ],
        out_specs=block(ROWS),
        compiler_params=pltpu.CompilerParams(vmem_limit_bytes=32 << 20),
        cost_estimate=cost(12 << 20, 4 << 30),
    )(windows, query, key_value, key_value)


def backward_kernel(windows, query, key, value, grad, mixed, dquery, dkey, dvalue, dbias):
    low = lax.broadcasted_iota(jnp.int32, (LENGTH, 128), 1) < SIZE
    keys, values = flat(key[0]), flat(value[0])
    all_queries = query[0].astype(F32).reshape(LENGTH, 128) * SIZE**-0.5
    all_grads = grad[0].astype(F32).reshape(LENGTH, 128)
    blocks = LENGTH // ROWS
    results = []
    for head in range(2):
        own = low if head == 0 else ~low
        queries = jnp.where(own, all_queries, 0.0).astype(BF16)
        grads = jnp.where(own, all_grads, 0.0).astype(BF16)
        bias = jnp.concatenate(
            [bias_rows(windows[0, head, block : block + 1]) for block in range(blocks)], 0
        )
        probs = softmax(dot(queries, keys, NT) + bias)
        low_probs = probs.astype(BF16)
        dprobs = dot(grads, values, NT)
        dscores = probs * (dprobs - jnp.sum(probs * dprobs, -1, keepdims=True))
        low_scores = dscores.astype(BF16)
        results.append(
            (
                dot(low_probs, values),
                dot(low_scores, keys) * SIZE**-0.5,
                dot(low_scores, queries, TN),
                dot(low_probs, grads, TN),
            )
        )
        diagonal = jnp.zeros((1, 1024), F32)
        for block in range(blocks):
            sums = jnp.concatenate(
                [
                    low_scores[block * ROWS : block * ROWS + ROWS].astype(F32),
                    jnp.zeros((ROWS, 128), F32),
                ],
                axis=1,
            )
            count = ROWS
            while count > 1:
                count //= 2
                sums = pltpu.roll(sums[:count], count, 1) + sums[count:]
            first = LENGTH - ROWS - block * ROWS
            pieces = [sums]
            if first:
                pieces.insert(0, jnp.zeros((1, first), F32))
            if first + 640 < 1024:
                pieces.append(jnp.zeros((1, 1024 - 640 - first), F32))
            diagonal = diagonal + jnp.concatenate(pieces, axis=1)
        dbias[0, 0, head : head + 1] = diagonal
    for ref, one, two in zip((mixed, dquery, dkey, dvalue), *results):
        ref[0] = tiled(jnp.where(low, one, two))


def attend_back(windows, query, key, value, grad):
    block = pl.BlockSpec((1, LENGTH // 8, 8, 128), lambda pair, item: (item, 0, 0, pair))
    shape = jax.ShapeDtypeStruct((2, LENGTH // 8, 8, 256), BF16)
    return pl.pallas_call(
        backward_kernel,
        grid=(2, 2),
        out_shape=(shape,) * 4 + (jax.ShapeDtypeStruct((2, 2, 2, 1024), F32),),
        in_specs=[
            pl.BlockSpec((1, 2, 4, 640), lambda pair, item: (pair, 0, 0, 0)),
            block,
            block,
            block,
            block,
        ],
        out_specs=(block,) * 4
        + (pl.BlockSpec((1, 1, 2, 1024), lambda pair, item: (item, pair, 0, 0)),),
        compiler_params=pltpu.CompilerParams(vmem_limit_bytes=48 << 20),
        cost_estimate=cost(12 << 20, 8 << 30),
    )(windows, query, key, value, grad)


def rows_of(packets):
    count, width = packets.shape[0], packets.shape[-1]
    return packets.astype(F32).reshape(count * 16, width).astype(BF16)


def packets_of(rows):
    return rows.astype(F32).reshape(rows.shape[0] // 16, 2, 8, rows.shape[1]).astype(BF16)


def expert_rows(rows, grads, gates, gate_w, up_w, down_w, dgate, dup, ddown):
    gate_pre = dot(rows, gate_w[...], NT)
    up_pre = dot(rows, up_w[...], NT)
    square = gate_pre * gate_pre
    root = math.sqrt(2 / math.pi)
    tanh = jnp.tanh(root * gate_pre * (1.0 + 0.044715 * square))
    half = 0.5 * (1.0 + tanh)
    value = gate_pre * half
    slope = half + (0.5 * root) * gate_pre * (1.0 - tanh * tanh) * (1.0 + 3 * 0.044715 * square)
    active = (value * up_pre).astype(BF16)
    out = dot(active, down_w[...])
    grads = grads.astype(F32)
    grad_gates = jnp.sum(out * grads, -1, keepdims=True)
    grad_out = (gates * grads).astype(BF16)
    grad_active = dot(grad_out, down_w[...], NT)
    grad_gate = (grad_active * up_pre * slope).astype(BF16)
    grad_up = (grad_active * value).astype(BF16)
    grad_rows = dot(grad_gate, gate_w[...]) + dot(grad_up, up_w[...])
    dgate[...] += dot(grad_gate, rows, TN)
    dup[...] += dot(grad_up, rows, TN)
    ddown[...] += dot(active, grad_out, TN)
    return out.astype(BF16), grad_rows.astype(BF16), grad_gates


def moe_kernel(
    main,
    tail,
    grads,
    gate_w,
    up_w,
    down_w,
    back_main,
    back_tail,
    outs,
    dgate,
    dup,
    ddown,
    own_main,
    own_tail,
    sib_main,
    sib_tail,
    grad_held,
    res_held,
    part_main,
    part_tail,
    give_main,
    give_tail,
    got_main,
    got_tail,
    keep_sem,
    send,
    recv,
    near_send,
    near_recv,
    grad_sem,
    res_sem,
    give_send,
    give_recv,
    back_keep,
    back_send,
    back_recv,
):
    x, y, z, core = place()
    my_dp = device(x, y, z, core)[0]
    sibling = device(x, y, z, 1 - core)
    greet_chips()
    slabs, own, sib = (main, tail), (own_main, own_tail), (sib_main, sib_tail)
    part, give, got = (part_main, part_tail), (give_main, give_tail), (got_main, got_tail)
    back = (back_main, back_tail)
    per = 8

    def packet(k):
        to = device(*chips(k)[0], core)
        return [
            remote(slabs[i].at[to[0]], own[i].at[k], send.at[i, k], recv.at[i, k], to)
            for i in range(2)
        ]

    def keep():
        return [
            pltpu.make_async_copy(slabs[i].at[my_dp], own[i].at[0], keep_sem.at[i])
            for i in range(2)
        ]

    def share(k):
        return [
            remote(own[i].at[k], sib[i].at[k], near_send.at[i, k], near_recv.at[i, k], sibling)
            for i in range(2)
        ]

    def arrive(block):
        @pl.loop(0, per)
        def _(j):
            k = block * per + j

            @pl.when(k > 0)
            def _():
                for copy in packet(k):
                    copy.wait_recv()

            for copy in share(k):
                copy.start()

    def fetches(block, j):
        slot = rem(block, 2)
        copies = []
        for side in range(2):
            dp, seq = device(*chips(block * per + j)[1], core if side == 0 else 1 - core)
            spot = side * per + j
            copies.append(
                pltpu.make_async_copy(
                    grads.at[seq, dp], grad_held.at[slot, spot], grad_sem.at[slot, spot]
                )
            )
        return copies

    def results(block, j):
        slot = rem(block, 2)
        copies = []
        for side in range(2):
            dp, seq = device(*chips(block * per + j)[1], core if side == 0 else 1 - core)
            spot = side * per + j
            copies.append(
                pltpu.make_async_copy(
                    res_held.at[slot, spot], outs.at[seq, dp], res_sem.at[slot, spot]
                )
            )
        return copies

    def each(copies, block, act):
        @pl.loop(0, per)
        def _(j):
            for copy in copies(block, j):
                act(copy)

    def hand(block):
        some = pl.ds(block * per, per)
        return [
            remote(
                give[i].at[some],
                got[i].at[some],
                give_send.at[i, block],
                give_recv.at[i, block],
                sibling,
            )
            for i in range(2)
        ]

    def reply(k):
        to = device(*chips(k)[1], core)
        return [
            remote(
                part[i].at[k], back[i].at[div(x, 2), my_dp], back_send.at[i, k], back_recv.at[i, k], to
            )
            for i in range(2)
        ]

    def keep_back():
        return [
            pltpu.make_async_copy(
                part[i].at[0], back[i].at[div(x, 2), my_dp], back_keep.at[i]
            )
            for i in range(2)
        ]

    def finish(block):
        for copy in hand(block):
            copy.wait_recv()

        @pl.loop(0, per)
        def _(j):
            k = block * per + j
            for i in range(2):
                part[i][k] = (part[i][k].astype(F32) + got[i][k].astype(F32)).astype(BF16)

            @pl.when(k > 0)
            def _():
                for copy in reply(k):
                    copy.start()

            @pl.when(k == 0)
            def _():
                for copy in keep_back():
                    copy.start()

    def work(block):
        slot = rem(block, 2)
        some = pl.ds(block * per, per)
        target = lax.broadcasted_iota(jnp.int32, (64, 256), 0)
        source = lax.broadcasted_iota(jnp.int32, (64, 256), 1)
        picks = [(source == 4 * target + m).astype(F32).astype(BF16) for m in range(4)]

        def whole(extra):
            return jnp.concatenate([dot(pick, extra).astype(BF16) for pick in picks], 1)

        def quarters(rows):
            pieces = [
                dot(picks[m], rows[:, 256 * m : 256 * m + 256], TN) for m in range(4)
            ]
            return pieces[0] + pieces[1] + pieces[2] + pieces[3]

        tails = jnp.concatenate([rows_of(own_tail[some]), rows_of(sib_tail[some])], 0)
        rows = jnp.concatenate(
            [rows_of(own_main[some]), rows_of(sib_main[some]), whole(tails[:, :256])], 0
        )
        held = rows_of(grad_held[slot])
        row_grads = jnp.concatenate([held[:, :D], whole(held[:, D:])], 0)
        scalars = jnp.concatenate([tails[:, 256:].astype(F32), dot(picks[0], tails[:, 256:])], 0)
        first = lax.broadcasted_iota(jnp.int32, (320, 1), 0) < 256
        gates = jnp.where(
            first,
            scalars[:, 0:1] + scalars[:, 1:2],
            scalars[:, 2:3] + scalars[:, 3:4],
        )
        out, grad_rows, grad_gates = expert_rows(
            rows, row_grads, gates, gate_w, up_w, down_w, dgate, dup, ddown
        )
        res_held[slot] = packets_of(
            jnp.concatenate([out[:256], quarters(out[256:]).astype(BF16)], 1)
        )
        lane = lax.broadcasted_iota(jnp.int32, (320, 128), 1)
        lanes = jnp.where(lane == jnp.where(first, 0, 1), grad_gates, 0.0)
        extra_lanes = lanes[256:].astype(BF16)
        aux = lanes[:256] + (
            dot(picks[0], extra_lanes, TN)
            + dot(picks[1], extra_lanes, TN)
            + dot(picks[2], extra_lanes, TN)
            + dot(picks[3], extra_lanes, TN)
        )
        ends = jnp.concatenate([quarters(grad_rows[256:]), aux], 1)
        part_main[some] = packets_of(grad_rows[:128])
        give_main[some] = packets_of(grad_rows[128:256])
        part_tail[some] = packets_of(ends[:128])
        give_tail[some] = packets_of(ends[128:])

    for copy in keep():
        copy.start()

    @pl.loop(1, 64)
    def _(k):
        for copy in packet(k):
            copy.start()

    each(fetches, 0, lambda copy: copy.start())
    dgate[...] = jnp.zeros_like(dgate)
    dup[...] = jnp.zeros_like(dup)
    ddown[...] = jnp.zeros_like(ddown)
    for copy in keep():
        copy.wait()
    arrive(0)
    blocks = 64 // per

    @pl.loop(0, blocks)
    def _(block):
        @pl.when(block < blocks - 1)
        def _():
            each(fetches, block + 1, lambda copy: copy.start())
            arrive(block + 1)

        @pl.loop(0, per)
        def _(j):
            for copy in share(block * per + j):
                copy.wait_recv()

        each(fetches, block, lambda copy: copy.wait())

        @pl.when(block >= 2)
        def _():
            each(results, block - 2, lambda copy: copy.wait())

        work(block)
        each(results, block, lambda copy: copy.start())
        for copy in hand(block):
            copy.start()

        @pl.when(block >= 1)
        def _():
            finish(block - 1)

    finish(blocks - 1)
    for block in (blocks - 2, blocks - 1):
        each(results, block, lambda copy: copy.wait())

    @pl.loop(0, blocks)
    def _(block):
        for copy in hand(block):
            copy.wait_send()

    @pl.loop(0, 64)
    def _(k):
        for copy in share(k):
            copy.wait_send()

        @pl.when(k > 0)
        def _():
            for copy in packet(k):
                copy.wait_send()
            for copy in reply(k):
                copy.wait_recv()
                copy.wait_send()

    for copy in keep_back():
        copy.wait()


def run_experts(main, tail, grads, gate_w, up_w, down_w):
    wide = gate_w.shape[0]
    grad = jax.ShapeDtypeStruct((wide, D), F32)

    def pair(count):
        return [pltpu.VMEM((count, 2, 8, D), BF16), pltpu.VMEM((count, 2, 8, TAIL), BF16)]

    staged = [pltpu.VMEM((2, 16, 2, 8, PACK), BF16)]
    return pl.pallas_call(
        moe_kernel,
        out_shape=(
            jax.ShapeDtypeStruct((2, 32, 2, 8, D), BF16),
            jax.ShapeDtypeStruct((2, 32, 2, 8, TAIL), BF16),
            jax.ShapeDtypeStruct((4, 32, 2, 8, PACK), BF16),
            grad,
            grad,
            grad,
        ),
        in_specs=[ANY] * 3 + [VMEM] * 3,
        out_specs=(ANY,) * 3 + (VMEM,) * 3,
        scratch_shapes=pair(64)
        + pair(64)
        + staged
        + staged
        + pair(64)
        + pair(64)
        + pair(64)
        + [DMA((2,))]
        + [DMA((2, 64))] * 4
        + [DMA((2, 16))] * 2
        + [DMA((2, 8))] * 2
        + [DMA((2,))]
        + [DMA((2, 64))] * 2,
        compiler_params=params(2, 60),
        cost_estimate=cost(90 << 20, 33 << 30),
    )(main, tail, grads, gate_w, up_w, down_w)


def rms_forward(values, gain):
    factor = lax.rsqrt(jnp.mean(values * values, -1, keepdims=True) + EPSILON)
    normed = values * factor
    return (normed, factor, normed * gain)


def rms_values(grad_output, normed, factor, gain):
    grad_normed = grad_output * gain
    return factor * (grad_normed - normed * jnp.mean(grad_normed * normed, -1, keepdims=True))


def split(values):
    high = values.astype(BF16)
    return high, (values - high.astype(F32)).astype(BF16)


def body(
    layer_in,
    w_query,
    w_key,
    w_value,
    w_out,
    norm_attn,
    norm_moe,
    rel_table,
    w_router,
    expert_gate,
    expert_up,
    expert_down,
    routes,
    rel_bucket,
    cotangent,
):
    tokens = 2 * ROWS
    seq = lax.axis_index("seq")

    route_flat = routes.reshape(tokens, 2)
    expert_ids = jnp.arange(EXPERTS, dtype=jnp.int32)
    choose_hot = route_flat[:, :, None] == expert_ids[None, None, :]
    order_hot = choose_hot.transpose(1, 0, 2).reshape(2 * tokens, EXPERTS).astype(jnp.int32)
    earlier = jnp.cumsum(order_hot, 0) - order_hot
    slot_order = jnp.sum(earlier * order_hot, -1)
    dropped = jnp.sum(order_hot * (slot_order >= CAP)[:, None].astype(jnp.int32), 0)
    tallies = jnp.stack([jnp.sum(order_hot, 0), dropped])
    slots = slot_order.reshape(2, tokens).transpose(1, 0)
    columns = jnp.arange(EXPERTS * MAIN, dtype=jnp.int32)
    main_place = jnp.where(slots < MAIN, route_flat * MAIN + slots, -1)
    hot_main = main_place[:, :, None] == columns[None, None, :]
    extra_place = jnp.where(
        (slots >= MAIN) & (slots < CAP), route_flat * 4 + slots - MAIN, -1
    )
    hot_extra = extra_place[:, :, None] == columns[None, None, : EXPERTS * 4]
    hot_main_both = jnp.sum(hot_main.astype(BF16), 1)
    hot_extra_both = jnp.sum(hot_extra.astype(BF16), 1)

    def spread(values):
        main = dot(hot_main_both, values, TN).astype(BF16)
        extra = dot(hot_extra_both, values, TN).astype(BF16)
        return main, extra.reshape(EXPERTS * MAIN, 256)

    slab = jnp.concatenate(
        [
            w_query,
            w_key,
            w_value,
            w_out,
            w_router,
            norm_attn[:, None],
            norm_moe[:, None],
            jnp.pad(rel_table[None], ((0, 7), (0, 0))),
            jnp.pad(tallies.astype(BF16), ((0, 6), (0, 0))),
            jnp.zeros((8, 186), BF16),
        ],
        1,
    )
    grad_main, grad_extra = spread(cotangent.reshape(tokens, D))
    full, items, route_grads = gather_all(
        slab,
        layer_in.reshape(2, 16, 8, D),
        jnp.concatenate([grad_main, grad_extra], 1).reshape(EXPERTS, 2, 8, PACK),
    )

    full = full.reshape(D, SLAB)
    full_query, full_kv, full_out = full[:, :D], full[:, D : 3 * D], full[:, 3 * D : 4 * D]
    smalls = full[:, 4 * D :]
    full_router = smalls[:, 0:32]
    gain_attn = smalls[:, 32].astype(F32)
    gain_moe = smalls[:, 33].astype(F32)
    smalls = smalls.reshape(128, 8, 256)
    table = smalls[:, 0, 34:38].reshape(BUCKETS, HEADS)
    totals = jnp.sum(smalls[:, 0:2, 38:70].astype(F32), 0).astype(jnp.int32)

    inputs = layer_in.astype(F32).reshape(tokens, D)
    own_hidden = rms_forward(inputs, gain_attn)[2].astype(BF16)
    all_inputs = items.astype(F32).reshape(4 * tokens, D)
    normed_one, factor_one, hidden_one = rms_forward(all_inputs, gain_attn)
    hidden_one = hidden_one.astype(BF16)
    query = dot(own_hidden, full_query).astype(BF16)
    kv_all = dot(hidden_one, full_kv).astype(BF16)
    bucket_hot = (rel_bucket[:, None] == jnp.arange(BUCKETS, dtype=jnp.int32)[None, :]).astype(BF16)
    offsets = jnp.einsum("ob,bh->ho", bucket_hot, table, preferred_element_type=F32)
    offsets = jnp.pad(offsets, ((0, 0), (0, 1)))
    windows = lax.dynamic_slice(offsets, (0, LENGTH - ROWS - seq * ROWS), (HEADS, 640))
    mixed = attend(
        windows.reshape(HEADS // 2, 2, 640),
        query.reshape(2, ROWS // 8, 8, D),
        kv_all.reshape(2, LENGTH // 8, 8, 2 * D),
    ).reshape(tokens, D)
    resid = inputs + dot(mixed, full_out)
    normed_two, factor_two, hidden_two = rms_forward(resid, gain_moe)
    hidden_two = hidden_two.astype(BF16)
    logits = dot(hidden_two, full_router)
    chosen = jnp.sum(jnp.where(choose_hot, logits[:, None, :], 0.0), -1)
    gates = jax.nn.softmax(chosen, -1)

    rows_main, rows_extra = spread(hidden_two)
    gate_main = jnp.sum(jnp.where(hot_main, gates[:, :, None], 0.0), (0, 1))
    gate_extra = jnp.sum(jnp.where(hot_extra, gates[:, :, None], 0.0), (0, 1))
    gate_extra = jnp.repeat(gate_extra, 4)
    lanes = jnp.stack(split(gate_main) + split(gate_extra), -1)
    rows_tail = jnp.concatenate([rows_extra, jnp.pad(lanes, ((0, 0), (0, 124)))], -1)
    route_grads = lax.all_gather(route_grads, "seq", axis=0, tiled=False)
    returned, returned_tail, outs, *expert_grads = run_experts(
        rows_main.reshape(EXPERTS, 2, 8, D),
        rows_tail.reshape(EXPERTS, 2, 8, TAIL),
        route_grads,
        expert_gate[0].T,
        expert_up[0].T,
        expert_down[0],
    )
    grad_gate, grad_up, grad_down = expert_grads[0].T, expert_grads[1].T, expert_grads[2]

    back_tail = returned_tail.reshape(2 * EXPERTS * MAIN, TAIL)
    back_extra = back_tail[:, :256].reshape(2 * EXPERTS * 4, D)
    grad_from_experts = dot(
        jnp.concatenate([hot_main_both, hot_main_both], 1), returned.reshape(2 * EXPERTS * MAIN, D)
    ) + dot(jnp.concatenate([hot_extra_both, hot_extra_both], 1), back_extra)
    returned_gates = back_tail[:, 256:258].astype(F32).reshape(2, EXPERTS * MAIN, 2)
    returned_gates = returned_gates[0] + returned_gates[1]
    extra_gates = returned_gates[:, 1].reshape(EXPERTS * 4, 4)[:, 0]
    grad_gates = jnp.sum(jnp.where(hot_main, returned_gates[:, 0], 0.0), -1) + jnp.sum(
        jnp.where(hot_extra, extra_gates, 0.0), -1
    )

    grad_final = cotangent.astype(F32).reshape(tokens, D)
    grad_chosen = gates * (grad_gates - jnp.sum(gates * grad_gates, -1, keepdims=True))
    grad_logits = jnp.sum(jnp.where(choose_hot, grad_chosen[:, :, None], 0.0), 1).astype(BF16)
    grad_router_part = dot(hidden_two, grad_logits, TN)
    grad_hidden_two = grad_from_experts + dot(grad_logits, full_router, NT)
    grad_gain_moe = jnp.sum(grad_hidden_two * normed_two, 0)
    grad_resid = grad_final + rms_values(grad_hidden_two, normed_two, factor_two, gain_moe)
    grad_attended = gather_items(grad_resid.astype(BF16).reshape(2, 16, 8, D))
    grad_attended, outs = lax.optimization_barrier((grad_attended, outs))
    outs = lax.psum_scatter(outs, "seq", scatter_dimension=0, tiled=False)
    grad_attended = grad_attended.reshape(4 * tokens, D)

    first = seq * 256
    own_query, own_key, own_value = [
        lax.dynamic_slice(full, (0, index * D + first), (D, 256)) for index in range(3)
    ]
    own_out = lax.dynamic_slice(full, (first, 3 * D), (256, D))
    head_query = dot(hidden_one, own_query).astype(BF16)
    head_key = lax.dynamic_slice(kv_all, (0, first), (4 * tokens, 256))
    head_value = lax.dynamic_slice(kv_all, (0, D + first), (4 * tokens, 256))
    grad_mixed = dot(grad_attended, own_out, NT).astype(BF16)
    head_offsets = lax.dynamic_slice(offsets, (seq * 4, 0), (4, 1024))
    head_windows = jnp.stack(
        [
            head_offsets[:, LENGTH - ROWS - block * ROWS : LENGTH - ROWS - block * ROWS + 640]
            for block in range(4)
        ],
        1,
    ).reshape(2, 2, 4, 640)
    shape = (2, LENGTH // 8, 8, 256)
    head_mixed, dquery, dkey, dvalue, dbias = attend_back(
        head_windows,
        head_query.reshape(shape),
        head_key.reshape(shape),
        head_value.reshape(shape),
        grad_mixed.reshape(shape),
    )
    grad_offsets = jnp.sum(dbias, 0).reshape(4, 1024)[:, :1023]
    grad_table = jnp.einsum(
        "ob,ho->bh", bucket_hot.astype(F32), grad_offsets, precision=lax.Precision.HIGHEST
    )
    heads_grad = jnp.concatenate([dquery, dkey, dvalue], -1).reshape(4 * tokens, 768)
    own_weights = jnp.concatenate([own_query, own_key, own_value], 1)
    grad_qkv = dot(hidden_one, heads_grad, TN).astype(BF16).reshape(32, 32, 768)
    grad_out = dot(head_mixed.reshape(4 * tokens, 256), grad_attended, TN).astype(BF16)
    grad_out = grad_out.reshape(32, 8, 4, 256).transpose(0, 2, 1, 3).reshape(32, 32, 256)
    part_hidden = dot(heads_grad, own_weights, NT)
    grad_gain_attn = jnp.sum(part_hidden * normed_one, 0)
    table_lanes = (
        (jnp.arange(32, dtype=jnp.int32) == seq * 8)[None, :, None] * grad_table[:, None, :]
    )
    smalls_grad = jnp.concatenate(
        [
            grad_router_part.reshape(32, 32, 32),
            grad_gain_attn.reshape(32, 32, 1),
            grad_gain_moe.reshape(32, 32, 1),
            table_lanes,
            jnp.zeros((32, 32, 90), F32),
        ],
        -1,
    ).astype(BF16)
    rest = jnp.concatenate([smalls_grad, grad_out], -1)
    mine, other, small_sums, wide_sums, outs = reduce_grads(
        grad_qkv.reshape(4, 2, 4, 4, 8, 768),
        rest.reshape(4, 2, 4, 4, 8, 384),
        part_hidden.astype(BF16).reshape(2, 4, 16, 8, D),
        outs,
    )

    gated_main = split(jnp.sum(jnp.where(hot_main, gates[:, :, None], 0.0), 1))
    gated_extra = split(jnp.sum(jnp.where(hot_extra, gates[:, :, None], 0.0), 1))
    outs = outs.reshape(EXPERTS * MAIN, PACK)
    out_main, out_extra = outs[:, :D], outs[:, D:].reshape(EXPERTS * 4, D)
    moe_out = (
        dot(gated_main[0], out_main)
        + dot(gated_main[1], out_main)
        + dot(gated_extra[0], out_extra)
        + dot(gated_extra[1], out_extra)
    )
    layer_out = (resid + moe_out).astype(BF16).reshape(2, ROWS, D)


    wide_sums = wide_sums.transpose(1, 0, 2).reshape(8, D)
    moves = [
        (dp * 4 + own, (8 * own + dp // 4) * 4 + dp % 4) for dp in range(32) for own in range(4)
    ]
    grad_out_own = lax.ppermute(wide_sums, ("dp", "seq"), moves)
    grad_weights = [
        small_sums[:, :, index * 256 : index * 256 + 256].transpose(1, 0, 2).reshape(8, D)
        for index in range(3)
    ]
    small_own = jnp.sum(small_sums[:, :, 768:], 0)
    grad_hidden_one = (mine + other.astype(F32)).reshape(tokens, D)
    own_normed, own_factor, _ = rms_forward(inputs, gain_attn)
    grad_in = grad_resid + rms_values(grad_hidden_one, own_normed, own_factor, gain_attn)
    return (
        layer_out,
        grad_in.reshape(2, ROWS, D),
        grad_weights[0],
        grad_weights[1],
        grad_weights[2],
        grad_out_own,
        small_own[:, 32],
        small_own[:, 33],
        small_own[0, 34:38],
        small_own[:, 0:32],
        grad_gate[None],
        grad_up[None],
        grad_down[None],
        totals,
    )


def solution(mesh):
    rows = P(("dp", "seq"), None)
    vector = P(("dp", "seq"))
    block = P("dp", "seq", None)
    wide = P("dp", None, "seq")
    return jax.shard_map(
        body,
        mesh=mesh,
        in_specs=(
            block,
            rows,
            rows,
            rows,
            rows,
            vector,
            vector,
            vector,
            rows,
            wide,
            wide,
            block,
            block,
            P(),
            block,
        ),
        out_specs=(
            block,
            block,
            rows,
            rows,
            rows,
            rows,
            vector,
            vector,
            vector,
            rows,
            wide,
            wide,
            block,
            P(),
        ),
        check_vma=False,
    )
```
